32 devices in a mesh: groups: 2 (over x), wide: 4 (over y, core), narrow: 4 (over z).
Axes of the slice: x: 2, y: 2, z: 4, core: 2. Of those that a mesh axis runs over, the one named last changes fastest.
Arguments:
- coeffs: bfloat16 [16, 2, 512, 1536], P(('groups', 'wide'), None, 'narrow'), parts along dimension 0, may hold values from -0.109375 to 0.109375
- energies: bfloat16 [16, 512], P(('groups', 'wide'), 'narrow'), parts along dimension 0, may hold values from 1.59375 to 2.59375
- g_coupling: bfloat16 [16, 64, 936], P(('groups', 'narrow')), parts along dimension 0, may hold values from -0.75 to 0.75
- omega: float32 [16, 9], P('groups'), parts along dimension 0, may hold values from 0.02 to 0.2
- pairs: int32 [32, 2], P(('groups', 'wide')), parts along dimension 0, may hold values from 0 to 7, as said below
- counts: int32 [8], P('groups'), parts along dimension 0, may hold values from 1 to 4, 8 in all
- blocks: int32 [16, 512], P(('groups', 'wide')), parts along dimension 0, may hold values from 0 to 511, as said below
Outputs:
- linewidth: float32 [16, 512], P(('groups', 'wide'), 'narrow'), parts along dimension 0
The draws below stay inside these ranges and needn't reach their ends.
There are 2 independent parts, one for each index of `groups`. The reference program is written for one: setup_inputs(seed, part) draws one part's arguments, and reference() takes and returns one part's arrays. A program takes and returns all parts, laid end to end along the dimension named above; each array names one. Nothing has to cross between parts.
Inputs may be any that keep to these rules, and one draw needn't show every extreme that they name: Worker w's rows are w * 4 to (w + 1) * 4 - 1; its live pairs are its first counts[w] rows. Each row's Q lies in w * 2 to (w + 1) * 2 - 1. Among one worker's 4 rows the owner ((Q + q) mod 8) // 2 takes any value at most 1 times, and some value exactly 1 times. Each exciton's label is the index of the first exciton of its degenerate block; blocks are 1 to 4 consecutive excitons, and some block holds exactly 4.
All inputs are finite; a program needn't handle non-finite values.
Results may differ from the reference program's by a relative error of at most 0.0003.
Values may be sent and summed in bfloat16 or wider, within the bound.
A program may use at most 192 MiB of HBM per device.

```python
import math
import jax
import jax.numpy as jnp
import numpy as np
from jax import lax

EXCITONS = 512
MODES = 9
CBANDS = 6
VBANDS = 4
KWIN = 64
QDEV = 2
PDEV = 4
TRANS = 1536
GWIDTH = 936
NQ = 8
PAIRS = 16
LIVE = 8
COLS = 128
N_WIDE = 4


def draw_pairs(key, part):
    key = jax.random.fold_in(key, 7)
    first_key, second_key, third_key = jax.random.split(key, 3)
    workers = PAIRS // PDEV
    orders = jax.vmap(lambda item: jax.random.permutation(item, workers))(jax.random.split(first_key, workers))
    slot_number = jnp.arange(PDEV) % workers
    far_owner = orders[:, slot_number]
    home_local = jax.random.randint(second_key, (workers, PDEV), 0, QDEV)
    far_local = jax.random.randint(third_key, (workers, PDEV), 0, QDEV)
    home_index = jnp.arange(workers)[:, None] * QDEV + home_local
    far_index = far_owner * QDEV + far_local
    shift_index = (far_index - home_index) % NQ
    return jnp.stack([home_index, shift_index], axis=-1).reshape(PAIRS, 2).astype(jnp.int32)


def draw_blocks(key, part):
    key = jax.random.fold_in(key, 11)
    flips = jax.random.randint(key, (NQ, EXCITONS), 0, 2)
    position = jnp.arange(EXCITONS)
    local = position % COLS
    starts = jnp.where(position % 2 == 0, 1, flips)
    upper_zone = (local >= COLS - 2) & (position < EXCITONS - COLS)
    lower_zone = (local <= 1) & (position >= COLS)
    zone = upper_zone | lower_zone
    forced = (local == COLS - 2).astype(jnp.int32)
    starts = jnp.where(zone[None, :], forced[None, :], starts)
    starts = jnp.where((position == EXCITONS - 1)[None, :], 1, starts)
    marks = jnp.where(starts == 1, position[None, :], 0).astype(jnp.int32)
    return lax.cummax(marks, axis=1).astype(jnp.int32)


def steps_of(rng, shape, cuts, low, high):
    level, own = 1.0, jax.random.fold_in(rng, 6)
    for dim, shards_of in cuts:
        steps = jnp.exp(jax.random.uniform(jax.random.fold_in(own, dim), (shards_of,), jnp.float32, low / len(cuts), high / len(cuts)))
        level = level * jnp.repeat(steps, shape[dim] // shards_of).reshape([-1 if axis == dim else 1 for axis in range(len(shape))])
    return level


def length_profile(number_of, total, limit, lean):
    loads = [(1 << 20) // math.isqrt(grade ** lean) + 1 for grade in range(2, number_of + 1)]
    rest, given = total - limit - (number_of - 1), [1] * (number_of - 1)
    while rest > 0:
        free = [i for i in range(number_of - 1) if given[i] < limit]
        pool, budget = sum([loads[i] for i in free]), rest
        for i in free:
            addition = min(limit - given[i], max(1, budget * loads[i] // pool), rest)
            given[i] = given[i] + addition
            rest = rest - addition
    return np.array([limit] + given)


def uneven(rng, amount, total, most, slope):
    if amount == 2:
        one = jax.random.randint(rng, (), max(1, total - most), min(most, total - 1) + 1)
        return jnp.stack([one, total - one])
    sizes = jnp.asarray(length_profile(amount, total, most, slope), jnp.int32)
    couples = (amount - 1) // 2
    giver, taker = sizes[1:1 + 2 * couples:2], sizes[2:2 + 2 * couples:2]
    margin = jnp.minimum(giver - 1, most - taker)
    passed = jax.random.randint(jax.random.fold_in(rng, 1), (couples,), 0, 1 << 20) % (margin + 1)
    sizes = sizes.at[1:1 + 2 * couples:2].set(giver - passed).at[2:2 + 2 * couples:2].set(taker + passed)
    return sizes[jax.random.permutation(jax.random.fold_in(rng, 2), amount)]


def centred(own_key, dims, spread, bound, pieces=(), kind=jnp.bfloat16):
    drawn = jax.random.normal(own_key, dims, jnp.float32) * spread
    if len(pieces) > 0:
        drawn = steps_of(own_key, dims, pieces, -0.22, 0.18) * drawn
    return jnp.clip(drawn, min=-bound, max=bound).astype(kind)


def setup_inputs(seed: int = 0, part: int = 0) -> dict:
    keys = jax.random.split(jax.random.key(seed), 8)
    own_keys = jax.random.split(jax.random.fold_in(keys[7], part), 8)
    return {
        "coeffs": centred(own_keys[0], (NQ, 2, EXCITONS, TRANS), (2 * TRANS) ** -0.5, 0.109375, ((0, 4), (2, 4))),
        "energies": jnp.clip(1.59375 + 1.0 * jax.random.uniform(own_keys[1], (NQ, EXCITONS), jnp.float32) ** steps_of(own_keys[1], (NQ, EXCITONS), ((0, 4), (1, 4)), -0.2, 0.2), 1.59375, 2.59375).astype(jnp.bfloat16),
        "g_coupling": centred(own_keys[2], (NQ, KWIN, GWIDTH), 64 ** -0.5, 0.75, ((0, 4),)),
        "omega": jnp.clip(jax.random.uniform(own_keys[3], (NQ, MODES), jnp.float32, 0.02, 0.2), 0.02, 0.2),
        "pairs": draw_pairs(jax.random.fold_in(jax.random.fold_in(keys[7], part), 71), part),
        "counts": uneven(own_keys[5], N_WIDE, LIVE, PDEV, 2).astype(jnp.int32),
        "blocks": draw_blocks(jax.random.fold_in(jax.random.fold_in(keys[7], part), 71), part),
    }


broadening = 0.1


def pair_rate(own_rows, own_levels, far_rows, far_levels, coupling_row, frequency):
    cut_point = 2 * MODES * CBANDS * CBANDS
    coupling_row = coupling_row.astype(jnp.float32)
    electron = coupling_row[:, :cut_point].reshape(KWIN, 2, MODES, CBANDS, CBANDS)
    hole_part = coupling_row[:, cut_point:].reshape(KWIN, 2, MODES, VBANDS, VBANDS)
    real_rows = own_rows[0].astype(jnp.float32).reshape(EXCITONS, KWIN, CBANDS, VBANDS)
    imag_rows = own_rows[1].astype(jnp.float32).reshape(EXCITONS, KWIN, CBANDS, VBANDS)

    def by_electron(gain, rows):
        return jnp.einsum("kucd,nkdv->unkcv", gain, rows)

    def by_hole(gain, rows):
        return jnp.einsum("kuvw,nkcw->unkcv", gain, rows)

    elec_real, elec_imag = electron[:, 0], electron[:, 1]
    hole_real, hole_imag = hole_part[:, 0], hole_part[:, 1]
    real_out = by_electron(elec_real, real_rows) - by_electron(elec_imag, imag_rows) - by_hole(hole_real, real_rows) + by_hole(hole_imag, imag_rows)
    imag_out = by_electron(elec_real, imag_rows) + by_electron(elec_imag, real_rows) - by_hole(hole_real, imag_rows) - by_hole(hole_imag, real_rows)
    real_mix = lax.optimization_barrier(real_out.reshape(MODES, EXCITONS, TRANS).astype(jnp.bfloat16)).astype(jnp.float32)
    imag_mix = lax.optimization_barrier(imag_out.reshape(MODES, EXCITONS, TRANS).astype(jnp.bfloat16)).astype(jnp.float32)
    far_real = far_rows[0].astype(jnp.float32)
    far_imag = far_rows[1].astype(jnp.float32)
    coupled_real = jnp.einsum("mx,unx->umn", far_real, real_mix) + jnp.einsum("mx,unx->umn", far_imag, imag_mix)
    coupled_imag = jnp.einsum("mx,unx->umn", far_real, imag_mix) - jnp.einsum("mx,unx->umn", far_imag, real_mix)
    power = coupled_real * coupled_real + coupled_imag * coupled_imag
    detuning = far_levels.astype(jnp.float32)[None, :, None] - own_levels.astype(jnp.float32)[None, None, :] - frequency[:, None, None]
    weight = 1.0 / (1.0 + (detuning / broadening) ** 2)
    return jnp.sum(power * weight, axis=(0, 1))


def reference(coeffs, energies, g_coupling, omega, pairs, counts, blocks):
    home_index = pairs[:, 0]
    shift_index = pairs[:, 1]
    far_index = (home_index + shift_index) % NQ
    slot_number = jnp.arange(PAIRS, dtype=jnp.int32) % PDEV
    worker_number = jnp.arange(PAIRS, dtype=jnp.int32) // PDEV
    active = (slot_number < counts[worker_number]).astype(jnp.float32)

    def one_pair(total, index):
        home = home_index[index]
        far = far_index[index]
        shift = shift_index[index]
        rate = pair_rate(coeffs[home], energies[home], coeffs[far], energies[far], g_coupling[shift], omega[shift])
        return total.at[home].add(active[index] * rate), None

    total = lax.scan(one_pair, jnp.zeros((NQ, EXCITONS), jnp.float32), jnp.arange(PAIRS, dtype=jnp.int32))[0]

    def average(items):
        values, labels = items
        same = (labels[:, None] == labels[None, :]).astype(jnp.float32)
        return jnp.sum(same * values[None, :], axis=1) / jnp.sum(same, axis=1)

    return lax.map(average, (total, blocks))
```

```python
import functools

import jax
import jax.numpy as jnp
import numpy as np
from jax import lax
from jax.experimental import pallas as pl
from jax.experimental.pallas import tpu as pltpu
from jax.sharding import PartitionSpec as P

MODES = 9
CBANDS = 6
VBANDS = 4
BANDS = CBANDS * VBANDS
ROWS = MODES * 2 * BANDS

broadening = 0.1


def expansion_tables():
    u, pout, c, v = np.unravel_index(np.arange(ROWS), (MODES, 2, CBANDS, VBANDS))
    cut = 2 * MODES * CBANDS * CBANDS
    index, mask = [], []
    for pin in range(2):
        part = pout ^ pin
        sign = np.where((pout == 0) & (pin == 1), -1.0, 1.0)
        for d in range(CBANDS):
            index.append(((part * MODES + u) * CBANDS + c) * CBANDS + d)
            mask.append(np.stack([sign * (v == other) for other in range(VBANDS)]))
    electron_mask = np.stack(mask)
    mask = []
    for pin in range(2):
        part = pout ^ pin
        sign = np.where((pout == 0) & (pin == 1), 1.0, -1.0)
        for w in range(VBANDS):
            index.append(cut + ((part * MODES + u) * VBANDS + v) * VBANDS + w)
            mask.append(np.stack([sign * (c == other) for other in range(CBANDS)]))
    hole_mask = np.stack(mask)
    return np.stack(index).astype(np.int32), electron_mask, hole_mask


def expand_coupling(chosen):
    index, electron_mask, hole_mask = expansion_tables()
    share, kpoints, width = chosen.shape
    entries = index.shape[0]
    select = (jnp.arange(width, dtype=jnp.int32)[:, None] == jnp.asarray(index).reshape(1, -1)).astype(chosen.dtype)
    picked = jnp.dot(chosen.reshape(share * kpoints, width), select)
    picked = picked.reshape(share, kpoints, entries, ROWS)
    cut = 2 * CBANDS
    electron = picked[:, :, :cut, None, :] * jnp.asarray(electron_mask, chosen.dtype)
    hole = picked[:, :, cut:, None, :] * jnp.asarray(hole_mask, chosen.dtype)
    return jnp.concatenate(
        [
            electron.reshape(share, kpoints, 2 * BANDS, ROWS),
            hole.reshape(share, kpoints, 2 * BANDS, ROWS),
        ],
        axis=2,
    )


def rate_kernel(omega_ref, gain_ref, own_ref, far_ref, own_e_ref, far_e_ref, rate_ref, mixed):
    pair = pl.program_id(0)
    kpoints = gain_ref.shape[1]
    columns = own_ref.shape[-1]
    trans = kpoints * BANDS

    def mix(step, carry):
        parts = []
        for offset in range(2):
            k = step * 2 + offset
            parts.append(
                lax.dot_general(
                    gain_ref[0, k], own_ref[0, k], (((0,), (0,)), ((), ())), preferred_element_type=jnp.float32
                )
            )
        start = pl.multiple_of(step * 2 * BANDS, 2 * BANDS)
        for u in range(MODES):
            for p in range(2):
                low = (u * 2 + p) * BANDS
                both = jnp.concatenate([part[low : low + BANDS] for part in parts], axis=0)
                mixed[u, pl.ds(start, 2 * BANDS), p * columns : (p + 1) * columns] = both.astype(jnp.bfloat16)
        return carry

    lax.fori_loop(0, kpoints // 2, mix, 0)
    far_real = far_ref[:, 0, 0].reshape(-1, trans)
    far_imag = far_ref[:, 0, 1].reshape(-1, trans)
    gap = far_e_ref[0] - own_e_ref[0]

    def mode(u, total):
        first = mixed[u]
        second = jnp.concatenate([first[:, columns:], -first[:, :columns]], axis=1)
        coupled = jnp.dot(far_real, first, preferred_element_type=jnp.float32)
        coupled += jnp.dot(far_imag, second, preferred_element_type=jnp.float32)
        real, imag = coupled[:, :columns], coupled[:, columns:]
        scaled = (gap - omega_ref[pair, u]) / broadening
        power = (real * real + imag * imag) / (1.0 + scaled * scaled)
        return total + jnp.sum(power, axis=0, keepdims=True)

    rate_ref[0] = lax.fori_loop(0, MODES, mode, jnp.zeros((1, columns), jnp.float32))


def pair_rates(omega, gain, own, far, own_e, far_e):
    share, kpoints, depth, rows = gain.shape
    columns = own.shape[-1]
    parts, trans = far.shape[0], far.shape[-1]
    excitons = parts * far.shape[3]
    flops = 2 * share * (kpoints * depth * rows * columns + excitons * 4 * trans * MODES * columns)
    return pl.pallas_call(
        rate_kernel,
        grid=(share,),
        in_specs=[
            pl.BlockSpec(memory_space=pltpu.SMEM),
            pl.BlockSpec((1, kpoints, depth, rows), lambda i: (i, 0, 0, 0)),
            pl.BlockSpec((1, kpoints, depth, columns), lambda i: (i, 0, 0, 0)),
            pl.BlockSpec((parts, 1, 2, far.shape[3], trans), lambda i: (0, i, 0, 0, 0)),
            pl.BlockSpec((1, 1, columns), lambda i: (i, 0, 0)),
            pl.BlockSpec((1, excitons, 1), lambda i: (i, 0, 0)),
        ],
        out_specs=pl.BlockSpec((1, 1, columns), lambda i: (i, 0, 0)),
        out_shape=jax.ShapeDtypeStruct((share, 1, columns), jnp.float32),
        scratch_shapes=[pltpu.VMEM((MODES, trans, 2 * columns), jnp.bfloat16)],
        compiler_params=pltpu.CompilerParams(vmem_limit_bytes=56 * 1024 * 1024),
        cost_estimate=pl.CostEstimate(flops=flops, bytes_accessed=2 * (gain.size + own.size + far.size), transcendentals=0),
    )(omega, gain, own, far, own_e, far_e)


def shards(coeffs, energies, g_coupling, omega, pairs, counts, blocks):
    worker = lax.axis_index("wide")
    part = lax.axis_index("narrow")
    workers = lax.axis_size("wide")
    owned, _, columns, trans = coeffs.shape
    kpoints = g_coupling.shape[1]
    momenta = owned * workers
    slots = pairs.shape[0]
    excitons = blocks.shape[1]

    small = jnp.concatenate([energies.astype(jnp.float32).reshape(-1), pairs.astype(jnp.float32).reshape(-1)])
    small = lax.all_gather(small, ("wide", "narrow"), axis=0, tiled=False)
    small = small.reshape(workers, -1, small.shape[-1])
    levels = small[:, :, : owned * columns].reshape(workers, -1, owned, columns)
    levels = levels.transpose(0, 2, 1, 3).reshape(momenta, excitons)
    all_pairs = small[:, 0, owned * columns :].astype(jnp.int32).reshape(workers * slots, 2)

    ends = jnp.sum(jnp.where(jnp.arange(workers)[:, None] <= jnp.arange(workers)[None, :], counts[:, None], 0), axis=0)
    live = jnp.arange(momenta)
    holder = jnp.sum((ends[None, :] <= live[:, None]).astype(jnp.int32), axis=1)
    holder = jnp.minimum(holder, workers - 1)
    slot = holder * slots + live - (jnp.take(ends, holder) - jnp.take(counts, holder))
    live_pairs = jnp.take(all_pairs, jnp.clip(slot, 0, workers * slots - 1), axis=0)
    live_home = live_pairs[:, 0]
    mine = lax.dynamic_slice_in_dim(live_pairs, worker * owned, owned, 0)
    home, shift = mine[:, 0], mine[:, 1]
    far_index = (home + shift) % momenta

    tables = lax.all_gather(g_coupling, "narrow", axis=0, tiled=True)
    gain = expand_coupling(jnp.take(tables, shift, axis=0))
    frequency = jnp.take(omega, shift, axis=0)

    whole = lax.all_gather(coeffs, "wide", axis=0, tiled=True)
    far = lax.all_gather(jnp.take(whole, far_index, axis=0), "narrow", axis=0, tiled=False)
    own = jnp.take(whole, home, axis=0).reshape(owned, 2, columns, kpoints, CBANDS, VBANDS)
    by_electron = own.transpose(0, 3, 1, 4, 5, 2).reshape(owned, kpoints, 2 * BANDS, columns)
    by_hole = own.transpose(0, 3, 1, 5, 4, 2).reshape(owned, kpoints, 2 * BANDS, columns)
    own = jnp.concatenate([by_electron, by_hole], axis=2)

    own_e = lax.dynamic_slice_in_dim(jnp.take(levels, home, axis=0), part * columns, columns, 1)
    far_e = jnp.take(levels, far_index, axis=0)
    rates = pair_rates(frequency, gain, own, far, own_e[:, None, :], far_e[:, :, None])

    rates = lax.all_gather(rates.reshape(owned, columns), ("wide", "narrow"), axis=0, tiled=False)
    rates = rates.reshape(workers, -1, owned, columns).transpose(0, 2, 1, 3).reshape(momenta, excitons)
    local = worker * owned + jnp.arange(owned)
    chosen = (live_home[None, :] == local[:, None]).astype(jnp.float32)
    total = jnp.sum(chosen[:, :, None] * rates[None, :, :], axis=1)
    margin = 3
    widened = jnp.pad(total, ((0, 0), (margin, margin)))
    padded_labels = jnp.pad(blocks, ((0, 0), (margin, margin)), constant_values=-1)
    widened = lax.dynamic_slice_in_dim(widened, part * columns, columns + 2 * margin, 1)
    near_labels = lax.dynamic_slice_in_dim(padded_labels, part * columns, columns + 2 * margin, 1)
    my_labels = near_labels[:, margin : margin + columns]
    upper = jnp.zeros((owned, columns), jnp.float32)
    lower = jnp.zeros((owned, columns), jnp.float32)
    for offset in range(2 * margin + 1):
        same = (near_labels[:, offset : offset + columns] == my_labels).astype(jnp.float32)
        upper += same * widened[:, offset : offset + columns]
        lower += same
    return upper / lower


def solution(mesh):
    in_specs = (
        P(("groups", "wide"), None, "narrow", None),
        P(("groups", "wide"), "narrow"),
        P(("groups", "narrow"), None, None),
        P("groups", None),
        P(("groups", "wide"), None),
        P("groups"),
        P(("groups", "wide"), None),
    )
    out_specs = P(("groups", "wide"), "narrow")
    return jax.shard_map(shards, mesh=mesh, in_specs=in_specs, out_specs=out_specs, check_vma=False)
```

```python
import functools

import jax
import jax.numpy as jnp
import numpy as np
from jax import lax
from jax.experimental import pallas as pl
from jax.experimental.pallas import tpu as pltpu
from jax.sharding import PartitionSpec as P

MODES = 9
CBANDS = 6
VBANDS = 4
BANDS = CBANDS * VBANDS
ROWS = MODES * 2 * BANDS

broadening = 0.1
MESH = pl.DeviceIdType.MESH


def expansion_tables():
    u, pout, c, v = np.unravel_index(np.arange(ROWS), (MODES, 2, CBANDS, VBANDS))
    cut = 2 * MODES * CBANDS * CBANDS
    index, mask = [], []
    for pin in range(2):
        part = pout ^ pin
        sign = np.where((pout == 0) & (pin == 1), -1.0, 1.0)
        for d in range(CBANDS):
            index.append(((part * MODES + u) * CBANDS + c) * CBANDS + d)
            mask.append(np.stack([sign * (v == other) for other in range(VBANDS)]))
    electron_mask = np.stack(mask)
    mask = []
    for pin in range(2):
        part = pout ^ pin
        sign = np.where((pout == 0) & (pin == 1), 1.0, -1.0)
        for w in range(VBANDS):
            index.append(cut + ((part * MODES + u) * VBANDS + v) * VBANDS + w)
            mask.append(np.stack([sign * (c == other) for other in range(CBANDS)]))
    hole_mask = np.stack(mask)
    return np.stack(index).astype(np.int32), electron_mask, hole_mask


def spread_tables():
    electron = np.arange(2 * CBANDS * VBANDS) // VBANDS
    pin, _, w = np.unravel_index(np.arange(2 * CBANDS * VBANDS), (2, CBANDS, VBANDS))
    hole = 2 * CBANDS + pin * VBANDS + w
    source = np.concatenate([electron, hole])
    return (source[:, None] == np.arange(2 * (CBANDS + VBANDS))[None, :]).astype(np.float32)


def pick_coupling(chosen):
    index = expansion_tables()[0]
    share, kpoints, width = chosen.shape
    select = (jnp.arange(width, dtype=jnp.int32)[:, None] == jnp.asarray(index).reshape(1, -1)).astype(chosen.dtype)
    picked = jnp.dot(chosen.reshape(share * kpoints, width), select)
    return picked.reshape(share, kpoints, index.shape[0], ROWS)


def greet(workers, parts):
    worker, part = lax.axis_index("wide"), lax.axis_index("narrow")
    barrier = pltpu.get_barrier_semaphore()
    me = worker * parts + part
    total = workers * parts

    def hello(step, carry):
        other = lax.rem(me + step, total)
        pl.semaphore_signal(
            barrier, inc=1, device_id={"wide": other // parts, "narrow": lax.rem(other, parts)}, device_id_type=MESH
        )
        return carry

    lax.fori_loop(1, total, hello, 0)
    pl.semaphore_wait(barrier, total - 1)


def to_all(workers, parts, source, landing, send_sem, recv_sem, wait):
    worker, part = lax.axis_index("wide"), lax.axis_index("narrow")
    me = worker * parts + part
    total = workers * parts

    def one(step, carry):
        other = lax.rem(me + step, total)
        copy = pltpu.make_async_remote_copy(
            src_ref=source,
            dst_ref=landing.at[me],
            send_sem=send_sem.at[step],
            recv_sem=recv_sem.at[step],
            device_id={"wide": other // parts, "narrow": lax.rem(other, parts)},
            device_id_type=MESH,
        )
        if wait:
            copy.wait()
        else:
            copy.start()
        return carry

    lax.fori_loop(1, total, one, 0)


def exchange_kernel(workers, parts, small_ref, table_ref, small_out, table_out, smalls, tables, s_send, s_recv, t_send, t_recv):
    worker, part = lax.axis_index("wide"), lax.axis_index("narrow")
    me = worker * parts + part
    greet(workers, parts)
    to_all(workers, parts, small_ref, smalls, s_send, s_recv, False)
    copies = []
    for step in range(1, parts):
        copy = pltpu.make_async_remote_copy(
            src_ref=table_ref,
            dst_ref=tables.at[part],
            send_sem=t_send.at[step],
            recv_sem=t_recv.at[step],
            device_id={"narrow": lax.rem(part + step, parts)},
            device_id_type=MESH,
        )
        copy.start()
        copies.append(copy)
    smalls[me] = small_ref[...]
    tables[part] = table_ref[...]
    to_all(workers, parts, small_ref, smalls, s_send, s_recv, True)
    for copy in copies:
        copy.wait()
    small_out[...] = smalls[...]
    table_out[...] = tables[...]


def exchange(workers, parts, small, table):
    total = workers * parts
    return pl.pallas_call(
        functools.partial(exchange_kernel, workers, parts),
        in_specs=[pl.BlockSpec(memory_space=pltpu.VMEM)] * 2,
        out_specs=[pl.BlockSpec(memory_space=pltpu.VMEM)] * 2,
        out_shape=[
            jax.ShapeDtypeStruct((total,) + small.shape, small.dtype),
            jax.ShapeDtypeStruct((parts,) + table.shape, table.dtype),
        ],
        scratch_shapes=[
            pltpu.VMEM((total,) + small.shape, small.dtype),
            pltpu.VMEM((parts,) + table.shape, table.dtype),
            pltpu.SemaphoreType.DMA((total,)),
            pltpu.SemaphoreType.DMA((total,)),
            pltpu.SemaphoreType.DMA((parts,)),
            pltpu.SemaphoreType.DMA((parts,)),
        ],
        compiler_params=pltpu.CompilerParams(
            collective_id=0, has_side_effects=True, vmem_limit_bytes=24 * 1024 * 1024
        ),
        cost_estimate=pl.CostEstimate(flops=0, bytes_accessed=4 * parts * table.size, transcendentals=0),
    )(small, table)


def rate_kernel(
    workers, parts, omega_ref, picked_ref, spread_ref, mask_ref, own_ref, far_ref, own_e_ref, far_e_ref, out_ref,
    near, distant, mixed, rates, gathered, n_send, n_recv, m_send, m_recv, local_sem, r_send, r_recv,
):
    worker, part = lax.axis_index("wide"), lax.axis_index("narrow")
    me = worker * parts + part
    half = parts // 2
    side, place = part // half, lax.rem(part, half)
    share, kpoints = picked_ref.shape[:2]
    columns = own_ref.shape[-1]
    trans = kpoints * BANDS
    width = half * columns

    def near_copy(pair, i):
        return pltpu.make_async_remote_copy(
            src_ref=own_ref.at[pair],
            dst_ref=near.at[pair, place],
            send_sem=n_send.at[pair, i],
            recv_sem=n_recv.at[pair, place],
            device_id={"narrow": side * half + i},
            device_id_type=MESH,
        )

    def far_copy(pair, t):
        return pltpu.make_async_remote_copy(
            src_ref=far_ref.at[pair],
            dst_ref=distant.at[pair, lax.rem(part, 2)],
            send_sem=m_send.at[pair, t],
            recv_sem=m_recv.at[pair, lax.rem(part, 2)],
            device_id={"narrow": t * half + part // 2},
            device_id_type=MESH,
        )

    def near_self(pair):
        return pltpu.make_async_copy(own_ref.at[pair], near.at[pair, place], local_sem.at[pair, 0])

    def far_self(pair):
        return pltpu.make_async_copy(far_ref.at[pair], distant.at[pair, lax.rem(part, 2)], local_sem.at[pair, 1])

    greet(workers, parts)
    for pair in range(share):
        near_self(pair).start()
        for i in range(half):
            pl.when(side * half + i != part)(near_copy(pair, i).start)
        for t in range(2):
            target = t * half + part // 2
            pl.when(target != part)(far_copy(pair, t).start)
            pl.when(target == part)(far_self(pair).start)

    def one_pair(pair, carry):
        for i in range(half):

            @pl.when(side * half + i != part)
            def _():
                pltpu.make_async_remote_copy(
                    src_ref=own_ref.at[pair],
                    dst_ref=near.at[pair, i],
                    send_sem=n_send.at[pair, i],
                    recv_sem=n_recv.at[pair, i],
                    device_id={"narrow": side * half + i},
                    device_id_type=MESH,
                ).wait_recv()

        near_self(pair).wait()

        def mix(step, carry):
            blocks = []
            for offset in range(2):
                k = step * 2 + offset
                spread = jnp.dot(spread_ref[...], picked_ref[pair, k], preferred_element_type=jnp.float32)
                gain = spread.astype(jnp.bfloat16) * mask_ref[...]
                rows = jnp.concatenate([near[pair, i, k] for i in range(half)], axis=1)
                rows = jnp.concatenate([rows, rows], axis=0)
                blocks.append(
                    lax.dot_general(gain, rows, (((0,), (0,)), ((), ())), preferred_element_type=jnp.float32)
                )
            start = pl.multiple_of(step * 2 * BANDS, 2 * BANDS)
            for u in range(MODES):
                for p in range(2):
                    low = (u * 2 + p) * BANDS
                    both = jnp.concatenate([block[low : low + BANDS] for block in blocks], axis=0)
                    mixed[u, pl.ds(start, 2 * BANDS), p * width : (p + 1) * width] = both.astype(jnp.bfloat16)
            return carry

        lax.fori_loop(0, kpoints // 2, mix, 0)

        for s in range(2):

            @pl.when(place * 2 + s != part)
            def _():
                pltpu.make_async_remote_copy(
                    src_ref=far_ref.at[pair],
                    dst_ref=distant.at[pair, s],
                    send_sem=m_send.at[pair, s],
                    recv_sem=m_recv.at[pair, s],
                    device_id={"narrow": place * 2 + s},
                    device_id_type=MESH,
                ).wait_recv()

            pl.when(place * 2 + s == part)(far_self(pair).wait)

        far_rows = distant[pair].reshape(4 * columns, trans)
        gap = far_e_ref[pair] - own_e_ref[pair]

        def mode(u, total):
            coupled = jnp.dot(far_rows, mixed[u], preferred_element_type=jnp.float32)
            coupled = coupled.reshape(2, 2, columns, 2 * width)
            real = coupled[:, 0, :, :width] + coupled[:, 1, :, width:]
            imag = coupled[:, 0, :, width:] - coupled[:, 1, :, :width]
            scaled = (gap - omega_ref[pair, u]) / broadening
            power = (real * real + imag * imag).reshape(2 * columns, width) / (1.0 + scaled * scaled)
            return total + jnp.sum(power, axis=0, keepdims=True)

        rates[pair] = lax.fori_loop(0, MODES, mode, jnp.zeros((1, width), jnp.float32))
        return carry

    lax.fori_loop(0, share, one_pair, 0)
    gathered[me] = rates[...]
    to_all(workers, parts, rates, gathered, r_send, r_recv, False)
    for pair in range(share):
        for i in range(half):
            pl.when(side * half + i != part)(near_copy(pair, i).wait_send)
        for t in range(2):
            pl.when(t * half + part // 2 != part)(far_copy(pair, t).wait_send)
    to_all(workers, parts, rates, gathered, r_send, r_recv, True)
    out_ref[...] = gathered[...]


def pair_rates(workers, parts, omega, picked, own, far, own_e, far_e):
    share, kpoints = picked.shape[:2]
    columns = own.shape[-1]
    trans = far.shape[-1]
    total, width = workers * parts, parts // 2 * columns
    _, electron_mask, hole_mask = expansion_tables()
    hole_mask = hole_mask.reshape(2, VBANDS, CBANDS, ROWS).transpose(0, 2, 1, 3)
    mask = np.concatenate([electron_mask.reshape(2 * BANDS, ROWS), hole_mask.reshape(2 * BANDS, ROWS)])
    flops = 2 * share * (kpoints * 4 * BANDS * ROWS * width + 8 * columns * trans * MODES * width)
    vmem = pl.BlockSpec(memory_space=pltpu.VMEM)
    dma = pltpu.SemaphoreType.DMA
    return pl.pallas_call(
        functools.partial(rate_kernel, workers, parts),
        in_specs=[pl.BlockSpec(memory_space=pltpu.SMEM)] + [vmem] * 7,
        out_specs=vmem,
        out_shape=jax.ShapeDtypeStruct((total, share, 1, width), jnp.float32),
        scratch_shapes=[
            pltpu.VMEM((share, parts // 2) + own.shape[1:], own.dtype),
            pltpu.VMEM((share, 2) + far.shape[1:], far.dtype),
            pltpu.VMEM((MODES, trans, 2 * width), jnp.bfloat16),
            pltpu.VMEM((share, 1, width), jnp.float32),
            pltpu.VMEM((total, share, 1, width), jnp.float32),
            dma((share, parts // 2)),
            dma((share, parts // 2)),
            dma((share, 2)),
            dma((share, 2)),
            dma((share, 2)),
            dma((total,)),
            dma((total,)),
        ],
        compiler_params=pltpu.CompilerParams(
            collective_id=1, has_side_effects=True, vmem_limit_bytes=56 * 1024 * 1024
        ),
        cost_estimate=pl.CostEstimate(flops=flops, bytes_accessed=2 * (picked.size + own.size + far.size), transcendentals=0),
    )(omega, picked, jnp.asarray(spread_tables(), jnp.bfloat16), jnp.asarray(mask, jnp.bfloat16), own, far, own_e, far_e)


def shards(coeffs, energies, g_coupling, omega, pairs, counts, blocks):
    worker = lax.axis_index("wide")
    part = lax.axis_index("narrow")
    workers = lax.axis_size("wide")
    owned, _, columns, trans = coeffs.shape
    kpoints = g_coupling.shape[1]
    momenta = owned * workers
    slots = pairs.shape[0]
    excitons = blocks.shape[1]

    parts = lax.axis_size("narrow")
    small = jnp.concatenate([energies.astype(jnp.float32).reshape(-1), pairs.astype(jnp.float32).reshape(-1)])
    small = jnp.pad(small, (0, -small.shape[0] % 128)).reshape(1, -1)
    small, tables = exchange(workers, parts, small, g_coupling)
    small = small.reshape(workers, parts, small.shape[-1])
    tables = tables.reshape(momenta, kpoints, g_coupling.shape[-1])
    levels = small[:, :, : owned * columns].reshape(workers, -1, owned, columns)
    levels = levels.transpose(0, 2, 1, 3).reshape(momenta, excitons)
    all_pairs = small[:, 0, owned * columns : owned * columns + 2 * slots].astype(jnp.int32).reshape(workers * slots, 2)

    ends = jnp.sum(jnp.where(jnp.arange(workers)[:, None] <= jnp.arange(workers)[None, :], counts[:, None], 0), axis=0)
    live = jnp.arange(momenta)
    holder = jnp.sum((ends[None, :] <= live[:, None]).astype(jnp.int32), axis=1)
    holder = jnp.minimum(holder, workers - 1)
    slot = holder * slots + live - (jnp.take(ends, holder) - jnp.take(counts, holder))
    live_pairs = jnp.take(all_pairs, jnp.clip(slot, 0, workers * slots - 1), axis=0)
    live_home = live_pairs[:, 0]
    mine = lax.dynamic_slice_in_dim(live_pairs, worker * owned, owned, 0)
    home, shift = mine[:, 0], mine[:, 1]
    far_index = (home + shift) % momenta

    picked = pick_coupling(jnp.take(tables, shift, axis=0, mode="clip"))
    frequency = jnp.take(omega, shift, axis=0, mode="clip")

    whole = lax.all_gather(coeffs, "wide", axis=0, tiled=True)
    far = jnp.take(whole, far_index, axis=0, mode="clip")
    own = jnp.take(whole, home, axis=0, mode="clip").reshape(owned, 2, columns, kpoints, BANDS)
    own = own.transpose(0, 3, 1, 4, 2).reshape(owned, kpoints, 2 * BANDS, columns)

    half = parts // 2
    own_e = jnp.take(levels, home, axis=0, mode="clip")
    own_e = lax.dynamic_slice_in_dim(own_e, part // half * half * columns, half * columns, 1)
    far_e = jnp.take(levels, far_index, axis=0, mode="clip")
    far_e = lax.dynamic_slice_in_dim(far_e, part % half * 2 * columns, 2 * columns, 1)
    rates = pair_rates(workers, parts, frequency, picked, own, far, own_e[:, None, :], far_e[:, :, None])

    rates = rates.reshape(workers, 2, half, owned, half * columns).sum(axis=2)
    rates = rates.transpose(0, 2, 1, 3).reshape(momenta, excitons)
    local = worker * owned + jnp.arange(owned)
    chosen = (live_home[None, :] == local[:, None]).astype(jnp.float32)
    total = jnp.sum(chosen[:, :, None] * rates[None, :, :], axis=1)
    margin = 3
    widened = jnp.pad(total, ((0, 0), (margin, margin)))
    padded_labels = jnp.pad(blocks, ((0, 0), (margin, margin)), constant_values=-1)
    widened = lax.dynamic_slice_in_dim(widened, part * columns, columns + 2 * margin, 1)
    near_labels = lax.dynamic_slice_in_dim(padded_labels, part * columns, columns + 2 * margin, 1)
    my_labels = near_labels[:, margin : margin + columns]
    upper = jnp.zeros((owned, columns), jnp.float32)
    lower = jnp.zeros((owned, columns), jnp.float32)
    for offset in range(2 * margin + 1):
        same = (near_labels[:, offset : offset + columns] == my_labels).astype(jnp.float32)
        upper += same * widened[:, offset : offset + columns]
        lower += same
    return upper / lower


def solution(mesh):
    in_specs = (
        P(("groups", "wide"), None, "narrow", None),
        P(("groups", "wide"), "narrow"),
        P(("groups", "narrow"), None, None),
        P("groups", None),
        P(("groups", "wide"), None),
        P("groups"),
        P(("groups", "wide"), None),
    )
    out_specs = P(("groups", "wide"), "narrow")
    return jax.shard_map(shards, mesh=mesh, in_specs=in_specs, out_specs=out_specs, check_vma=False)
```

```python
import functools

import jax
import jax.numpy as jnp
import numpy as np
from jax import lax
from jax.experimental import pallas as pl
from jax.experimental.pallas import tpu as pltpu
from jax.sharding import PartitionSpec as P

MODES = 9
CBANDS = 6
VBANDS = 4
BANDS = CBANDS * VBANDS
ROWS = MODES * 2 * BANDS

broadening = 0.1
MESH = pl.DeviceIdType.MESH


LANES = 128
ENTRIES = 16
CHUNKS = 4


def compact_index():
    index = np.full((CBANDS + VBANDS, LANES), -1, np.int32)
    lane = np.arange(2 * MODES * CBANDS)
    for d in range(CBANDS):
        index[d, : lane.size] = lane * CBANDS + d
    lane = np.arange(2 * MODES * VBANDS)
    for w in range(VBANDS):
        index[CBANDS + w, : lane.size] = 2 * MODES * CBANDS * CBANDS + lane * VBANDS + w
    return index


def compact_tables(table):
    index = compact_index()
    count, kpoints, size = table.shape
    select = (jnp.arange(size, dtype=jnp.int32)[:, None] == jnp.asarray(index).reshape(1, -1)).astype(table.dtype)
    rows = jnp.dot(table.reshape(count * kpoints, size), select).reshape(count, kpoints, index.shape[0], LANES)
    rows = jnp.pad(rows, ((0, 0), (0, 0), (0, ENTRIES - index.shape[0]), (0, 0)))
    return rows.reshape(count, kpoints * ENTRIES, LANES)


def lane_tables():
    u, pout, c, v = np.unravel_index(np.arange(ROWS), (MODES, 2, CBANDS, VBANDS))
    padded_rows = -(-ROWS // LANES) * LANES
    electron = np.zeros((LANES, 2, padded_rows), np.float32)
    hole = np.zeros((LANES, 2, padded_rows), np.float32)
    for pin in range(2):
        part = pout ^ pin
        electron[(part * MODES + u) * CBANDS + c, pin, np.arange(ROWS)] = 1
        hole[(part * MODES + u) * VBANDS + v, pin, np.arange(ROWS)] = 1
    return electron.reshape(LANES, -1), hole.reshape(LANES, -1)


def spread_tables():
    u, pout, c, v = np.unravel_index(np.arange(ROWS), (MODES, 2, CBANDS, VBANDS))
    spread = np.zeros((4 * BANDS, 2 * ENTRIES), np.float32)
    mask = np.zeros((4 * BANDS, -(-ROWS // LANES) * LANES), np.float32)
    row = 0
    for hole in range(2):
        for pin in range(2):
            sign = np.where((pout == 0) & (pin == 1), -1.0, 1.0)
            for band in range(CBANDS):
                for other in range(VBANDS):
                    spread[row, pin * ENTRIES + (CBANDS + other if hole else band)] = 1
                    mask[row, :ROWS] = -sign * (c == band) if hole else sign * (v == other)
                    row += 1
    return spread, mask


def greet(workers, parts):
    worker, part = lax.axis_index("wide"), lax.axis_index("narrow")
    barrier = pltpu.get_barrier_semaphore()
    me = worker * parts + part
    total = workers * parts

    def hello(step, carry):
        other = lax.rem(me + step, total)
        pl.semaphore_signal(
            barrier, inc=1, device_id={"wide": other // parts, "narrow": lax.rem(other, parts)}, device_id_type=MESH
        )
        return carry

    lax.fori_loop(1, total, hello, 0)
    pl.semaphore_wait(barrier, total - 1)


def to_all(workers, parts, source, landing, send_sem, recv_sem, wait):
    worker, part = lax.axis_index("wide"), lax.axis_index("narrow")
    me = worker * parts + part
    total = workers * parts

    def one(step, carry):
        other = lax.rem(me + step, total)
        copy = pltpu.make_async_remote_copy(
            src_ref=source,
            dst_ref=landing.at[me],
            send_sem=send_sem.at[step],
            recv_sem=recv_sem.at[step],
            device_id={"wide": other // parts, "narrow": lax.rem(other, parts)},
            device_id_type=MESH,
        )
        if wait:
            copy.wait()
        else:
            copy.start()
        return carry

    lax.fori_loop(1, total, one, 0)


def exchange_kernel(workers, parts, small_ref, small_out, smalls, s_send, s_recv):
    worker, part = lax.axis_index("wide"), lax.axis_index("narrow")
    greet(workers, parts)
    to_all(workers, parts, small_ref, smalls, s_send, s_recv, False)
    smalls[worker * parts + part] = small_ref[...]
    to_all(workers, parts, small_ref, smalls, s_send, s_recv, True)
    small_out[...] = smalls[...]


def exchange(workers, parts, small):
    total = workers * parts
    return pl.pallas_call(
        functools.partial(exchange_kernel, workers, parts),
        in_specs=[pl.BlockSpec(memory_space=pltpu.VMEM)],
        out_specs=pl.BlockSpec(memory_space=pltpu.VMEM),
        out_shape=jax.ShapeDtypeStruct((total,) + small.shape, small.dtype),
        scratch_shapes=[
            pltpu.VMEM((total,) + small.shape, small.dtype),
            pltpu.SemaphoreType.DMA((total,)),
            pltpu.SemaphoreType.DMA((total,)),
        ],
        compiler_params=pltpu.CompilerParams(collective_id=0, has_side_effects=True),
    )(small)


def rate_kernel(
    workers, parts, index_ref, omega_ref, table_ref, coeffs_ref, electron_ref, hole_ref, spread_ref, mask_ref,
    own_e_ref, far_e_ref, out_ref, *scratch,
):
    wholes, scratch = scratch[:CHUNKS], scratch[CHUNKS:]
    (
        tables, picked, near, staged, distant, mixed, rates, gathered, w_send, w_recv, f_send, f_recv,
        t_send, t_recv, tf_send, tf_recv, n_send, n_recv, m_send, m_recv, r_send, r_recv,
    ) = scratch
    worker, part = lax.axis_index("wide"), lax.axis_index("narrow")
    me = worker * parts + part
    half, chips = parts // 2, workers // 2
    chip, core = worker // 2, lax.rem(worker, 2)
    partner = chip * 2 + 1 - core
    side, place = part // half, lax.rem(part, half)
    share = index_ref.shape[0]
    owned, _, columns, trans = coeffs_ref.shape
    chunk = trans // CHUNKS
    width = half * columns
    count = table_ref.shape[0]
    table_half = table_ref.shape[1] // 2
    steps = chunk // (2 * BANDS)

    def remote(src, dst, send, recv, device):
        return pltpu.make_async_remote_copy(
            src_ref=src, dst_ref=dst, send_sem=send, recv_sem=recv, device_id=device, device_id_type=MESH
        )

    def block(c, owner):
        return wholes[c].at[pl.ds(owner * owned, owned)]

    def wide_copy(c, hop):
        source = coeffs_ref.at[:, :, :, pl.ds(c * chunk, chunk)]
        target = partner if hop == 0 else lax.rem(chip + hop, chips) * 2 + core
        return remote(source, block(c, worker), w_send.at[c, hop], w_recv.at[c, hop], {"wide": target})

    def arrived(hop):
        return partner if hop == 0 else lax.rem(chip - hop + chips, chips) * 2 + core

    def wide_wait(c, hop):
        landing = block(c, arrived(hop))
        return remote(landing, landing, w_send.at[c, hop], w_recv.at[c, hop], {"wide": partner})

    def forward(c, hop):
        landing = block(c, arrived(hop))
        return remote(landing, landing, f_send.at[c, hop], f_recv.at[c, hop], {"wide": partner})

    def forward_wait(c, hop):
        landing = block(c, lax.rem(chip - hop + chips, chips) * 2 + 1 - core)
        return remote(landing, landing, f_send.at[c, hop], f_recv.at[c, hop], {"wide": partner})

    def table_rows(owner, which):
        start = pl.multiple_of(which * table_half, table_half)
        return tables.at[pl.ds(owner * count, count), pl.ds(start, table_half)]

    def table_copy(step):
        start = pl.multiple_of(core * table_half, table_half)
        return remote(
            table_ref.at[:, pl.ds(start, table_half)], table_rows(part, core), t_send.at[step], t_recv.at[step],
            {"narrow": lax.rem(part + step, parts)},
        )

    def table_arrival(step, which, send, recv):
        landing = table_rows(lax.rem(part - step + parts, parts), which)
        return remote(landing, landing, send.at[step], recv.at[step], {"wide": partner})

    def rows_of(c):
        return pl.ds(c * chunk, chunk)

    def near_copy(pair, c, i):
        ref = near.at[pair, place, :, rows_of(c)]
        return remote(ref, ref, n_send.at[pair, c, i], n_recv.at[pair, c, place], {"narrow": side * half + i})

    def near_wait(pair, c, i):
        ref = near.at[pair, i, :, rows_of(c)]
        return remote(ref, ref, n_send.at[pair, c, i], n_recv.at[pair, c, i], {"narrow": side * half + i})

    def far_copy(pair, c, t):
        slot = lax.rem(part, 2)
        return remote(
            staged.at[pair, :, :, rows_of(c)], distant.at[pair, slot, :, :, rows_of(c)],
            m_send.at[pair, c, t], m_recv.at[pair, c, slot], {"narrow": t * half + part // 2},
        )

    def far_wait(pair, c, s):
        ref = distant.at[pair, s, :, :, rows_of(c)]
        return remote(ref, ref, m_send.at[pair, c, s], m_recv.at[pair, c, s], {"narrow": place * 2 + s})

    def stage_near(pair, c):
        rows = wholes[c][index_ref[pair, 0]]
        for p in range(2):
            near[pair, place, p, rows_of(c)] = rows[p].T
        for i in range(half):
            pl.when(side * half + i != part)(near_copy(pair, c, i).start)

    def stage_far(pair, c):
        rows = wholes[c][index_ref[pair, 1]]
        staged[pair, :, :, rows_of(c)] = rows
        for t in range(2):
            target = t * half + part // 2
            pl.when(target != part)(far_copy(pair, c, t).start)

            @pl.when(target == part)
            def _():
                distant[pair, lax.rem(part, 2), :, :, rows_of(c)] = rows

    def pick(pair):
        size = 256
        lanes = 2 * mask_ref.shape[1]

        def some(step, carry):
            rows = pl.ds(pl.multiple_of(step * size, size), size)
            entries = tables[index_ref[pair, 2], rows]
            electron = jnp.dot(entries, electron_ref[...], preferred_element_type=jnp.float32)
            hole = jnp.dot(entries, hole_ref[...], preferred_element_type=jnp.float32)
            entry = lax.rem(lax.broadcasted_iota(jnp.int32, (size, lanes), 0), ENTRIES)
            picked[pair, rows] = jnp.where(entry < CBANDS, electron, hole).astype(jnp.bfloat16)
            return carry

        lax.fori_loop(0, table_ref.shape[1] // size, some, 0)

    def mix(pair, c):
        for i in range(half):
            pl.when(side * half + i != part)(near_wait(pair, c, i).wait_recv)
        lanes = mask_ref.shape[1]

        def some(step, carry):
            start = pl.multiple_of(step * 2 * BANDS, 2 * BANDS)
            whole_rows = [
                jnp.concatenate([near[pair, i, p, pl.ds(start, 2 * BANDS)] for i in range(half)], axis=1).astype(
                    jnp.float32
                )
                for p in range(2)
            ]
            blocks = []
            for offset in range(2):
                first = pl.multiple_of((step * 2 + offset) * ENTRIES, ENTRIES)
                entries = picked[pair, pl.ds(first, ENTRIES)]
                entries = jnp.concatenate([entries[:, :lanes], entries[:, lanes:]], axis=0)
                spread = jnp.dot(spread_ref[...], entries, preferred_element_type=jnp.float32)
                gain = (spread.astype(jnp.bfloat16) * mask_ref[...])[:, :ROWS]
                rows = jnp.concatenate([part_rows[offset * BANDS : (offset + 1) * BANDS] for part_rows in whole_rows], axis=0)
                rows = rows.astype(jnp.bfloat16)
                rows = jnp.concatenate([rows, rows], axis=0)
                blocks.append(
                    lax.dot_general(gain, rows, (((0,), (0,)), ((), ())), preferred_element_type=jnp.float32)
                )
            for u in range(MODES):
                for p in range(2):
                    low = (u * 2 + p) * BANDS
                    both = jnp.concatenate([one[low : low + BANDS] for one in blocks], axis=0)
                    mixed[u, pl.ds(start, 2 * BANDS), p * width : (p + 1) * width] = both.astype(jnp.bfloat16)
            return carry

        lax.fori_loop(c * steps, (c + 1) * steps, some, 0)

    def couple(pair):
        for c in range(CHUNKS):
            for s in range(2):
                pl.when(place * 2 + s != part)(far_wait(pair, c, s).wait_recv)
        far_rows = distant[pair].reshape(4 * columns, trans)
        gap = far_e_ref[pair] - own_e_ref[pair]

        def mode(u, total):
            coupled = jnp.dot(far_rows, mixed[u], preferred_element_type=jnp.float32)
            coupled = coupled.reshape(2, 2, columns, 2 * width)
            real = coupled[:, 0, :, :width] + coupled[:, 1, :, width:]
            imag = coupled[:, 0, :, width:] - coupled[:, 1, :, :width]
            scaled = (gap - omega_ref[pair, u]) / broadening
            power = (real * real + imag * imag).reshape(2 * columns, width) / (1.0 + scaled * scaled)
            return total + jnp.sum(power, axis=0, keepdims=True)

        rates[pair] = lax.fori_loop(0, MODES, mode, jnp.zeros((1, width), jnp.float32))

    greet(workers, parts)
    for c in range(CHUNKS):
        for hop in range(chips):
            wide_copy(c, hop).start()
    for step in range(1, parts):
        table_copy(step).start()
    for c in range(CHUNKS):
        wholes[c][pl.ds(worker * owned, owned)] = coeffs_ref[:, :, :, rows_of(c)]
    tables[pl.ds(part * count, count)] = table_ref[...]

    for c in range(CHUNKS):
        for hop in range(1, chips):
            wide_wait(c, hop).wait_recv()
            forward(c, hop).start()
        wide_wait(c, 0).wait_recv()
        for hop in range(1, chips):
            forward_wait(c, hop).wait_recv()
        stage_near(0, c)
        stage_far(0, c)
        if c == 0:
            for step in range(1, parts):
                table_arrival(step, core, t_send, t_recv).wait_recv()
                table_arrival(step, core, tf_send, tf_recv).start()
        if c == 1:
            for step in range(1, parts):
                table_arrival(step, 1 - core, tf_send, tf_recv).wait_recv()
            for pair in range(share):
                pick(pair)
        if c == 2:
            mix(0, 0)
    for pair in range(1, share):
        for c in range(CHUNKS):
            stage_near(pair, c)
        for c in range(CHUNKS):
            stage_far(pair, c)
    for c in range(1, CHUNKS):
        mix(0, c)
    couple(0)
    for pair in range(1, share):
        for c in range(CHUNKS):
            mix(pair, c)
        couple(pair)

    gathered[me] = rates[...]
    to_all(workers, parts, rates, gathered, r_send, r_recv, False)
    for c in range(CHUNKS):
        for hop in range(chips):
            wide_copy(c, hop).wait_send()
            if hop:
                forward(c, hop).wait_send()
        for pair in range(share):
            for i in range(half):
                pl.when(side * half + i != part)(near_copy(pair, c, i).wait_send)
            for t in range(2):
                pl.when(t * half + part // 2 != part)(far_copy(pair, c, t).wait_send)
    for step in range(1, parts):
        table_copy(step).wait_send()
        table_arrival(step, core, tf_send, tf_recv).wait_send()
    to_all(workers, parts, rates, gathered, r_send, r_recv, True)
    out_ref[...] = gathered[...]


def pair_rates(workers, parts, index, omega, table, coeffs, own_e, far_e):
    share = index.shape[0]
    owned, _, columns, trans = coeffs.shape
    total, half, chips = workers * parts, parts // 2, workers // 2
    width = half * columns
    electron, hole = lane_tables()
    spread, mask = spread_tables()
    constants = [jnp.asarray(one, jnp.bfloat16) for one in (electron, hole, spread, mask)]
    flops = 2 * share * (trans // BANDS * 4 * BANDS * ROWS * width + 8 * columns * trans * MODES * width)
    smem, vmem = pl.BlockSpec(memory_space=pltpu.SMEM), pl.BlockSpec(memory_space=pltpu.VMEM)
    dma, bf16 = pltpu.SemaphoreType.DMA, jnp.bfloat16
    return pl.pallas_call(
        functools.partial(rate_kernel, workers, parts),
        in_specs=[smem, smem] + [vmem] * 8,
        out_specs=vmem,
        out_shape=jax.ShapeDtypeStruct((total, share, 1, width), jnp.float32),
        scratch_shapes=[pltpu.VMEM((owned * workers, 2, columns, trans // CHUNKS), bf16)] * CHUNKS
        + [
            pltpu.VMEM((table.shape[0] * parts,) + table.shape[1:], bf16),
            pltpu.VMEM((share, table.shape[1], electron.shape[1]), bf16),
            pltpu.VMEM((share, half, 2, trans, columns), bf16),
            pltpu.VMEM((share, 2, columns, trans), bf16),
            pltpu.VMEM((share, 2, 2, columns, trans), bf16),
            pltpu.VMEM((MODES, trans, 2 * width), bf16),
            pltpu.VMEM((share, 1, width), jnp.float32),
            pltpu.VMEM((total, share, 1, width), jnp.float32),
        ]
        + [dma((CHUNKS, chips))] * 4
        + [dma((parts,))] * 4
        + [dma((share, CHUNKS, half))] * 2
        + [dma((share, CHUNKS, 2))] * 2
        + [dma((total,))] * 2,
        compiler_params=pltpu.CompilerParams(
            collective_id=1, has_side_effects=True, vmem_limit_bytes=60 * 1024 * 1024
        ),
        cost_estimate=pl.CostEstimate(flops=flops, bytes_accessed=4 * coeffs.size, transcendentals=0),
    )(index, omega, table, coeffs, *constants, own_e, far_e)


def shards(coeffs, energies, g_coupling, omega, pairs, counts, blocks):
    worker = lax.axis_index("wide")
    part = lax.axis_index("narrow")
    workers = lax.axis_size("wide")
    owned, _, columns, trans = coeffs.shape
    momenta = owned * workers
    slots = pairs.shape[0]
    excitons = blocks.shape[1]

    parts = lax.axis_size("narrow")
    small = jnp.concatenate([energies.astype(jnp.float32).reshape(-1), pairs.astype(jnp.float32).reshape(-1)])
    small = jnp.pad(small, (0, -small.shape[0] % 128)).reshape(1, -1)
    small = exchange(workers, parts, small)
    small = small.reshape(workers, parts, small.shape[-1])
    levels = small[:, :, : owned * columns].reshape(workers, -1, owned, columns)
    levels = levels.transpose(0, 2, 1, 3).reshape(momenta, excitons)
    all_pairs = small[:, 0, owned * columns : owned * columns + 2 * slots].astype(jnp.int32).reshape(workers * slots, 2)

    ends = jnp.sum(jnp.where(jnp.arange(workers)[:, None] <= jnp.arange(workers)[None, :], counts[:, None], 0), axis=0)
    live = jnp.arange(momenta)
    holder = jnp.sum((ends[None, :] <= live[:, None]).astype(jnp.int32), axis=1)
    holder = jnp.minimum(holder, workers - 1)
    slot = holder * slots + live - (jnp.take(ends, holder) - jnp.take(counts, holder))
    live_pairs = jnp.take(all_pairs, jnp.clip(slot, 0, workers * slots - 1), axis=0)
    live_home = live_pairs[:, 0]
    mine = lax.dynamic_slice_in_dim(live_pairs, worker * owned, owned, 0)
    home, shift = mine[:, 0], mine[:, 1]
    far_index = (home + shift) % momenta

    frequency = jnp.take(omega, shift, axis=0, mode="clip")
    index = jnp.stack([home, far_index, shift], axis=1)

    half = parts // 2
    own_e = jnp.take(levels, home, axis=0, mode="clip")
    own_e = lax.dynamic_slice_in_dim(own_e, part // half * half * columns, half * columns, 1)
    far_e = jnp.take(levels, far_index, axis=0, mode="clip")
    far_e = lax.dynamic_slice_in_dim(far_e, part % half * 2 * columns, 2 * columns, 1)
    rates = pair_rates(
        workers, parts, index, frequency, compact_tables(g_coupling), coeffs, own_e[:, None, :], far_e[:, :, None]
    )

    rates = rates.reshape(workers, 2, half, owned, half * columns).sum(axis=2)
    rates = rates.transpose(0, 2, 1, 3).reshape(momenta, excitons)
    local = worker * owned + jnp.arange(owned)
    chosen = (live_home[None, :] == local[:, None]).astype(jnp.float32)
    total = jnp.sum(chosen[:, :, None] * rates[None, :, :], axis=1)
    margin = 3
    widened = jnp.pad(total, ((0, 0), (margin, margin)))
    padded_labels = jnp.pad(blocks, ((0, 0), (margin, margin)), constant_values=-1)
    widened = lax.dynamic_slice_in_dim(widened, part * columns, columns + 2 * margin, 1)
    near_labels = lax.dynamic_slice_in_dim(padded_labels, part * columns, columns + 2 * margin, 1)
    my_labels = near_labels[:, margin : margin + columns]
    upper = jnp.zeros((owned, columns), jnp.float32)
    lower = jnp.zeros((owned, columns), jnp.float32)
    for offset in range(2 * margin + 1):
        same = (near_labels[:, offset : offset + columns] == my_labels).astype(jnp.float32)
        upper += same * widened[:, offset : offset + columns]
        lower += same
    return upper / lower


def solution(mesh):
    in_specs = (
        P(("groups", "wide"), None, "narrow", None),
        P(("groups", "wide"), "narrow"),
        P(("groups", "narrow"), None, None),
        P("groups", None),
        P(("groups", "wide"), None),
        P("groups"),
        P(("groups", "wide"), None),
    )
    out_specs = P(("groups", "wide"), "narrow")
    return jax.shard_map(shards, mesh=mesh, in_specs=in_specs, out_specs=out_specs, check_vma=False)
```

```python
import functools

import jax
import jax.numpy as jnp
import numpy as np
from jax import lax
from jax.experimental import pallas as pl
from jax.experimental.pallas import tpu as pltpu
from jax.sharding import PartitionSpec as P

MODES = 9
CBANDS = 6
VBANDS = 4
BANDS = CBANDS * VBANDS
ROWS = MODES * 2 * BANDS

broadening = 0.1
MESH = pl.DeviceIdType.MESH


LANES = 128
ENTRIES = 16
CHUNKS = 4


def compact_index():
    index = np.full((CBANDS + VBANDS, LANES), -1, np.int32)
    lane = np.arange(2 * MODES * CBANDS)
    for d in range(CBANDS):
        index[d, : lane.size] = lane * CBANDS + d
    lane = np.arange(2 * MODES * VBANDS)
    for w in range(VBANDS):
        index[CBANDS + w, : lane.size] = 2 * MODES * CBANDS * CBANDS + lane * VBANDS + w
    return index


def compact_tables(table):
    index = compact_index()
    count, kpoints, size = table.shape
    select = (jnp.arange(size, dtype=jnp.int32)[:, None] == jnp.asarray(index).reshape(1, -1)).astype(table.dtype)
    rows = jnp.dot(table.reshape(count * kpoints, size), select).reshape(count, kpoints, index.shape[0], LANES)
    return rows.reshape(count, kpoints * index.shape[0], LANES)


def pad_table():
    row = np.arange(ENTRIES * ENTRIES)
    kept = row % ENTRIES < CBANDS + VBANDS
    pad = np.zeros((row.size, ENTRIES * (CBANDS + VBANDS)), np.float32)
    pad[row[kept], (row // ENTRIES * (CBANDS + VBANDS) + row % ENTRIES)[kept]] = 1
    return pad


def lane_tables():
    u, pout, c, v = np.unravel_index(np.arange(ROWS), (MODES, 2, CBANDS, VBANDS))
    padded_rows = -(-ROWS // LANES) * LANES
    electron = np.zeros((LANES, 2, padded_rows), np.float32)
    hole = np.zeros((LANES, 2, padded_rows), np.float32)
    for pin in range(2):
        part = pout ^ pin
        electron[(part * MODES + u) * CBANDS + c, pin, np.arange(ROWS)] = 1
        hole[(part * MODES + u) * VBANDS + v, pin, np.arange(ROWS)] = 1
    return electron.reshape(LANES, -1), hole.reshape(LANES, -1)


def spread_tables():
    u, pout, c, v = np.unravel_index(np.arange(ROWS), (MODES, 2, CBANDS, VBANDS))
    spread = np.zeros((4 * BANDS, 2 * ENTRIES), np.float32)
    mask = np.zeros((4 * BANDS, -(-ROWS // LANES) * LANES), np.float32)
    row = 0
    for hole in range(2):
        for pin in range(2):
            sign = np.where((pout == 0) & (pin == 1), -1.0, 1.0)
            for band in range(CBANDS):
                for other in range(VBANDS):
                    spread[row, pin * ENTRIES + (CBANDS + other if hole else band)] = 1
                    mask[row, :ROWS] = -sign * (c == band) if hole else sign * (v == other)
                    row += 1
    return spread, mask


def greet(workers, parts):
    worker, part = lax.axis_index("wide"), lax.axis_index("narrow")
    barrier = pltpu.get_barrier_semaphore()
    me = worker * parts + part
    total = workers * parts

    def hello(step, carry):
        other = lax.rem(me + step, total)
        pl.semaphore_signal(
            barrier, inc=1, device_id={"wide": other // parts, "narrow": lax.rem(other, parts)}, device_id_type=MESH
        )
        return carry

    lax.fori_loop(1, total, hello, 0)
    pl.semaphore_wait(barrier, total - 1)


def to_all(workers, parts, source, landing, send_sem, recv_sem, wait):
    worker, part = lax.axis_index("wide"), lax.axis_index("narrow")
    me = worker * parts + part
    total = workers * parts

    def one(step, carry):
        other = lax.rem(me + step, total)
        copy = pltpu.make_async_remote_copy(
            src_ref=source,
            dst_ref=landing.at[me],
            send_sem=send_sem.at[step],
            recv_sem=recv_sem.at[step],
            device_id={"wide": other // parts, "narrow": lax.rem(other, parts)},
            device_id_type=MESH,
        )
        if wait:
            copy.wait()
        else:
            copy.start()
        return carry

    lax.fori_loop(1, total, one, 0)


def exchange_kernel(workers, parts, small_ref, small_out, smalls, s_send, s_recv):
    worker, part = lax.axis_index("wide"), lax.axis_index("narrow")
    greet(workers, parts)
    to_all(workers, parts, small_ref, smalls, s_send, s_recv, False)
    smalls[worker * parts + part] = small_ref[...]
    to_all(workers, parts, small_ref, smalls, s_send, s_recv, True)
    small_out[...] = smalls[...]


def exchange(workers, parts, small):
    total = workers * parts
    return pl.pallas_call(
        functools.partial(exchange_kernel, workers, parts),
        in_specs=[pl.BlockSpec(memory_space=pltpu.VMEM)],
        out_specs=pl.BlockSpec(memory_space=pltpu.VMEM),
        out_shape=jax.ShapeDtypeStruct((total,) + small.shape, small.dtype),
        scratch_shapes=[
            pltpu.VMEM((total,) + small.shape, small.dtype),
            pltpu.SemaphoreType.DMA((total,)),
            pltpu.SemaphoreType.DMA((total,)),
        ],
        compiler_params=pltpu.CompilerParams(collective_id=0, has_side_effects=True),
    )(small)


def rate_kernel(
    workers, parts, index_ref, omega_ref, table_ref, coeffs_ref, pad_ref, electron_ref, hole_ref, spread_ref,
    mask_ref, small_ref, out_ref, *scratch,
):
    wholes, scratch = scratch[:CHUNKS], scratch[CHUNKS:]
    (
        tables, picked, near, staged, distant, mixed, partial, rates, gathered, w_send, w_recv, f_send, f_recv,
        t_send, t_recv, tf_send, tf_recv, n_send, n_recv, m_send, m_recv, r_send, r_recv,
    ) = scratch
    worker, part = lax.axis_index("wide"), lax.axis_index("narrow")
    me = worker * parts + part
    half, chips = parts // 2, workers // 2
    chip, core = worker // 2, lax.rem(worker, 2)
    partner = chip * 2 + 1 - core
    side, place = part // half, lax.rem(part, half)
    share = index_ref.shape[0]
    owned, _, columns, trans = coeffs_ref.shape
    chunk = trans // CHUNKS
    width = half * columns
    count = table_ref.shape[0]
    table_half = table_ref.shape[1] // 2
    steps = chunk // (2 * BANDS)

    def remote(src, dst, send, recv, device):
        return pltpu.make_async_remote_copy(
            src_ref=src, dst_ref=dst, send_sem=send, recv_sem=recv, device_id=device, device_id_type=MESH
        )

    def block(c, owner):
        return wholes[c].at[pl.ds(owner * owned, owned)]

    def wide_copy(c, hop):
        source = coeffs_ref.at[:, :, :, pl.ds(c * chunk, chunk)]
        target = partner if hop == 0 else lax.rem(chip + hop, chips) * 2 + core
        return remote(source, block(c, worker), w_send.at[c, hop], w_recv.at[c, hop], {"wide": target})

    def arrived(hop):
        return partner if hop == 0 else lax.rem(chip - hop + chips, chips) * 2 + core

    def wide_wait(c, hop):
        landing = block(c, arrived(hop))
        return remote(landing, landing, w_send.at[c, hop], w_recv.at[c, hop], {"wide": partner})

    def forward(c, hop):
        landing = block(c, arrived(hop))
        return remote(landing, landing, f_send.at[c, hop], f_recv.at[c, hop], {"wide": partner})

    def forward_wait(c, hop):
        landing = block(c, lax.rem(chip - hop + chips, chips) * 2 + 1 - core)
        return remote(landing, landing, f_send.at[c, hop], f_recv.at[c, hop], {"wide": partner})

    def table_rows(owner, which):
        start = pl.multiple_of(which * table_half, table_half)
        return tables.at[pl.ds(owner * count, count), pl.ds(start, table_half)]

    def table_copy(step):
        start = pl.multiple_of(core * table_half, table_half)
        return remote(
            table_ref.at[:, pl.ds(start, table_half)], table_rows(part, core), t_send.at[step], t_recv.at[step],
            {"narrow": lax.rem(part + step, parts)},
        )

    def table_arrival(step, which, send, recv):
        landing = table_rows(lax.rem(part - step + parts, parts), which)
        return remote(landing, landing, send.at[step], recv.at[step], {"wide": partner})

    def rows_of(c):
        return pl.ds(c * chunk, chunk)

    def near_copy(pair, c, i):
        ref = near.at[pair, place, :, rows_of(c)]
        return remote(ref, ref, n_send.at[pair, c, i], n_recv.at[pair, c, place], {"narrow": side * half + i})

    def near_wait(pair, c, i):
        ref = near.at[pair, i, :, rows_of(c)]
        return remote(ref, ref, n_send.at[pair, c, i], n_recv.at[pair, c, i], {"narrow": side * half + i})

    def far_copy(pair, c, t):
        slot = lax.rem(part, 2)
        return remote(
            staged.at[pair, :, :, rows_of(c)], distant.at[pair, slot, :, :, rows_of(c)],
            m_send.at[pair, c, t], m_recv.at[pair, c, slot], {"narrow": t * half + part // 2},
        )

    def far_wait(pair, c, s):
        ref = distant.at[pair, s, :, :, rows_of(c)]
        return remote(ref, ref, m_send.at[pair, c, s], m_recv.at[pair, c, s], {"narrow": place * 2 + s})

    def stage_near(pair, c):
        rows = wholes[c][index_ref[pair, 0]]
        for p in range(2):
            near[pair, place, p, rows_of(c)] = rows[p].T
        for i in range(half):
            pl.when(side * half + i != part)(near_copy(pair, c, i).start)

    def stage_far(pair, c):
        rows = wholes[c][index_ref[pair, 1]]
        staged[pair, :, :, rows_of(c)] = rows
        for t in range(2):
            target = t * half + part // 2
            pl.when(target != part)(far_copy(pair, c, t).start)

            @pl.when(target == part)
            def _():
                distant[pair, lax.rem(part, 2), :, :, rows_of(c)] = rows

    def pick(pair):
        size, kept = pad_ref.shape
        lanes = 2 * mask_ref.shape[1]

        def some(step, carry):
            rows = pl.ds(pl.multiple_of(step * size, size), size)
            packed = tables[index_ref[pair, 2], pl.ds(pl.multiple_of(step * kept, kept), kept)]
            entries = jnp.dot(pad_ref[...], packed, preferred_element_type=jnp.float32).astype(jnp.bfloat16)
            electron = jnp.dot(entries, electron_ref[...], preferred_element_type=jnp.float32)
            hole = jnp.dot(entries, hole_ref[...], preferred_element_type=jnp.float32)
            entry = lax.rem(lax.broadcasted_iota(jnp.int32, (size, lanes), 0), ENTRIES)
            picked[pair, rows] = jnp.where(entry < CBANDS, electron, hole).astype(jnp.bfloat16)
            return carry

        lax.fori_loop(0, table_ref.shape[1] // kept, some, 0)

    def mix(pair, c):
        for i in range(half):
            pl.when(side * half + i != part)(near_wait(pair, c, i).wait_recv)
        lanes = mask_ref.shape[1]

        def some(step, carry):
            start = pl.multiple_of(step * 2 * BANDS, 2 * BANDS)
            whole_rows = [
                jnp.concatenate([near[pair, i, p, pl.ds(start, 2 * BANDS)] for i in range(half)], axis=1).astype(
                    jnp.float32
                )
                for p in range(2)
            ]
            blocks = []
            for offset in range(2):
                first = pl.multiple_of((step * 2 + offset) * ENTRIES, ENTRIES)
                entries = picked[pair, pl.ds(first, ENTRIES)]
                entries = jnp.concatenate([entries[:, :lanes], entries[:, lanes:]], axis=0)
                spread = jnp.dot(spread_ref[...], entries, preferred_element_type=jnp.float32)
                gain = (spread.astype(jnp.bfloat16) * mask_ref[...])[:, :ROWS]
                rows = jnp.concatenate([part_rows[offset * BANDS : (offset + 1) * BANDS] for part_rows in whole_rows], axis=0)
                rows = rows.astype(jnp.bfloat16)
                rows = jnp.concatenate([rows, rows], axis=0)
                blocks.append(
                    lax.dot_general(gain, rows, (((0,), (0,)), ((), ())), preferred_element_type=jnp.float32)
                )
            for u in range(MODES):
                for p in range(2):
                    low = (u * 2 + p) * BANDS
                    both = jnp.concatenate([one[low : low + BANDS] for one in blocks], axis=0)
                    mixed[u, pl.ds(start, 2 * BANDS), p * width : (p + 1) * width] = both.astype(jnp.bfloat16)
            return carry

        lax.fori_loop(c * steps, (c + 1) * steps, some, 0)

    def gap_of(pair):
        own = [small_ref[index_ref[pair, 3] + side * half + i, pl.ds(index_ref[pair, 4], 1)] for i in range(half)]
        own = jnp.concatenate(own, axis=1)
        far = []
        for s in range(2):
            row = small_ref[index_ref[pair, 5] + place * 2 + s, pl.ds(index_ref[pair, 6], 1)]
            column = jnp.broadcast_to(row, (columns, columns)).T
            far.append(jnp.concatenate([column] * half, axis=1))
        return jnp.concatenate(far, axis=0) - own

    def far_arrival(pair, first, last):
        for c in range(first, last):
            for s in range(2):
                pl.when(place * 2 + s != part)(far_wait(pair, c, s).wait_recv)

    def weigh(pair, u, coupled, gap):
        coupled = coupled.reshape(2, 2, columns, 2 * width)
        real = coupled[:, 0, :, :width] + coupled[:, 1, :, width:]
        imag = coupled[:, 0, :, width:] - coupled[:, 1, :, :width]
        scaled = (gap - omega_ref[index_ref[pair, 2], u]) / broadening
        power = (real * real + imag * imag).reshape(2 * columns, width) / (1.0 + scaled * scaled)
        return jnp.sum(power, axis=0, keepdims=True)

    def couple(pair):
        cut = trans // 2
        gap = gap_of(pair)
        far_arrival(pair, 0, CHUNKS // 2)

        def start(u, carry):
            far_rows = distant[pair, :, :, :, :cut].reshape(4 * columns, cut)
            partial[u] = jnp.dot(far_rows, mixed[u, :cut], preferred_element_type=jnp.float32)
            return carry

        lax.fori_loop(0, MODES, start, 0)
        far_arrival(pair, CHUNKS // 2, CHUNKS)

        def finish(u, total):
            far_rows = distant[pair, :, :, :, cut:].reshape(4 * columns, trans - cut)
            coupled = partial[u] + jnp.dot(far_rows, mixed[u, cut:], preferred_element_type=jnp.float32)
            return total + weigh(pair, u, coupled, gap)

        rates[pair] = lax.fori_loop(0, MODES, finish, jnp.zeros((1, width), jnp.float32))

    greet(workers, parts)
    for c in range(CHUNKS):
        for hop in range(chips):
            wide_copy(c, hop).start()
    for step in range(1, parts):
        table_copy(step).start()
    for c in range(CHUNKS):
        wholes[c][pl.ds(worker * owned, owned)] = coeffs_ref[:, :, :, rows_of(c)]
    tables[pl.ds(part * count, count)] = table_ref[...]

    for c in range(CHUNKS):
        for hop in range(1, chips):
            wide_wait(c, hop).wait_recv()
            forward(c, hop).start()
        wide_wait(c, 0).wait_recv()
        for hop in range(1, chips):
            forward_wait(c, hop).wait_recv()
        stage_near(0, c)
        stage_far(0, c)
        if c == 0:
            for step in range(1, parts):
                table_arrival(step, core, t_send, t_recv).wait_recv()
                table_arrival(step, core, tf_send, tf_recv).start()
        if c == 1:
            for step in range(1, parts):
                table_arrival(step, 1 - core, tf_send, tf_recv).wait_recv()
            for pair in range(share):
                pick(pair)
        if c == 2:
            mix(0, 0)
    for pair in range(1, share):
        for c in range(CHUNKS):
            stage_near(pair, c)
        for c in range(CHUNKS):
            stage_far(pair, c)
    for c in range(1, CHUNKS):
        mix(0, c)
    couple(0)
    for pair in range(1, share):
        for c in range(CHUNKS):
            mix(pair, c)
        couple(pair)

    gathered[me] = rates[...]
    to_all(workers, parts, rates, gathered, r_send, r_recv, False)
    for c in range(CHUNKS):
        for hop in range(chips):
            wide_copy(c, hop).wait_send()
            if hop:
                forward(c, hop).wait_send()
        for pair in range(share):
            for i in range(half):
                pl.when(side * half + i != part)(near_copy(pair, c, i).wait_send)
            for t in range(2):
                pl.when(t * half + part // 2 != part)(far_copy(pair, c, t).wait_send)
    for step in range(1, parts):
        table_copy(step).wait_send()
        table_arrival(step, core, tf_send, tf_recv).wait_send()
    to_all(workers, parts, rates, gathered, r_send, r_recv, True)
    out_ref[...] = gathered[...]


def pair_rates(workers, parts, index, omega, table, coeffs, small):
    share = index.shape[0]
    owned, _, columns, trans = coeffs.shape
    total, half, chips = workers * parts, parts // 2, workers // 2
    width = half * columns
    electron, hole = lane_tables()
    spread, mask = spread_tables()
    constants = [jnp.asarray(one, jnp.bfloat16) for one in (pad_table(), electron, hole, spread, mask)]
    flops = 2 * share * (trans // BANDS * 4 * BANDS * ROWS * width + 8 * columns * trans * MODES * width)
    smem, vmem = pl.BlockSpec(memory_space=pltpu.SMEM), pl.BlockSpec(memory_space=pltpu.VMEM)
    dma, bf16 = pltpu.SemaphoreType.DMA, jnp.bfloat16
    return pl.pallas_call(
        functools.partial(rate_kernel, workers, parts),
        in_specs=[smem, smem] + [vmem] * 8,
        out_specs=vmem,
        out_shape=jax.ShapeDtypeStruct((total, share, 1, width), jnp.float32),
        scratch_shapes=[pltpu.VMEM((owned * workers, 2, columns, trans // CHUNKS), bf16)] * CHUNKS
        + [
            pltpu.VMEM((table.shape[0] * parts,) + table.shape[1:], bf16),
            pltpu.VMEM((share, trans // BANDS * ENTRIES, electron.shape[1]), bf16),
            pltpu.VMEM((share, half, 2, trans, columns), bf16),
            pltpu.VMEM((share, 2, columns, trans), bf16),
            pltpu.VMEM((share, 2, 2, columns, trans), bf16),
            pltpu.VMEM((MODES, trans, 2 * width), bf16),
            pltpu.VMEM((MODES, 4 * columns, 2 * width), jnp.float32),
            pltpu.VMEM((share, 1, width), jnp.float32),
            pltpu.VMEM((total, share, 1, width), jnp.float32),
        ]
        + [dma((CHUNKS, chips))] * 4
        + [dma((parts,))] * 4
        + [dma((share, CHUNKS, half))] * 2
        + [dma((share, CHUNKS, 2))] * 2
        + [dma((total,))] * 2,
        compiler_params=pltpu.CompilerParams(
            collective_id=1, has_side_effects=True, vmem_limit_bytes=60 * 1024 * 1024
        ),
        cost_estimate=pl.CostEstimate(flops=flops, bytes_accessed=4 * coeffs.size, transcendentals=0),
    )(index, omega, table, coeffs, *constants, small)


def shards(coeffs, energies, g_coupling, omega, pairs, counts, blocks):
    worker = lax.axis_index("wide")
    part = lax.axis_index("narrow")
    workers = lax.axis_size("wide")
    owned, _, columns, trans = coeffs.shape
    momenta = owned * workers
    slots = pairs.shape[0]
    excitons = blocks.shape[1]

    parts = lax.axis_size("narrow")
    listed = jnp.pad(pairs.astype(jnp.float32).reshape(1, -1), ((0, 0), (0, columns - 2 * slots)))
    small = exchange(workers, parts, jnp.concatenate([energies.astype(jnp.float32), listed], axis=0))
    listed = small.reshape(workers, parts, owned + 1, columns)[:, 0, owned, : 2 * slots]
    listed = listed.reshape(workers, slots, 2)

    before = jnp.arange(workers)[:, None] > jnp.arange(workers)[None, :]
    rank = jnp.sum(jnp.where(before, counts[None, :], 0), axis=1)[:, None] + jnp.arange(slots)[None, :]
    rank = jnp.where(jnp.arange(slots)[None, :] < counts[:, None], rank, -1)

    def live_rows(wanted):
        hit = (rank[None, :, :] == wanted[:, None, None])[..., None]
        return jnp.sum(jnp.where(hit, listed[None], 0.0), axis=(1, 2)).astype(jnp.int32)

    mine = live_rows(worker * owned + jnp.arange(owned))
    home, shift = mine[:, 0], mine[:, 1]
    far_index = (home + shift) % momenta
    index = jnp.stack(
        [
            home, far_index, shift,
            home // owned * parts, home % owned, far_index // owned * parts, far_index % owned,
        ],
        axis=1,
    )
    rates = pair_rates(workers, parts, index, omega, compact_tables(g_coupling), coeffs, small)

    live_home = live_rows(jnp.arange(momenta))[:, 0]
    half = parts // 2
    rates = rates.reshape(workers, 2, half, owned, half * columns).sum(axis=2)
    rates = rates.transpose(0, 2, 1, 3).reshape(momenta, excitons)
    local = worker * owned + jnp.arange(owned)
    chosen = (live_home[None, :] == local[:, None]).astype(jnp.float32)
    total = jnp.sum(chosen[:, :, None] * rates[None, :, :], axis=1)
    margin = 3
    widened = jnp.pad(total, ((0, 0), (margin, margin)))
    padded_labels = jnp.pad(blocks, ((0, 0), (margin, margin)), constant_values=-1)
    widened = lax.dynamic_slice_in_dim(widened, part * columns, columns + 2 * margin, 1)
    near_labels = lax.dynamic_slice_in_dim(padded_labels, part * columns, columns + 2 * margin, 1)
    my_labels = near_labels[:, margin : margin + columns]
    upper = jnp.zeros((owned, columns), jnp.float32)
    lower = jnp.zeros((owned, columns), jnp.float32)
    for offset in range(2 * margin + 1):
        same = (near_labels[:, offset : offset + columns] == my_labels).astype(jnp.float32)
        upper += same * widened[:, offset : offset + columns]
        lower += same
    return upper / lower


def solution(mesh):
    in_specs = (
        P(("groups", "wide"), None, "narrow", None),
        P(("groups", "wide"), "narrow"),
        P(("groups", "narrow"), None, None),
        P("groups", None),
        P(("groups", "wide"), None),
        P("groups"),
        P(("groups", "wide"), None),
    )
    out_specs = P(("groups", "wide"), "narrow")
    return jax.shard_map(shards, mesh=mesh, in_specs=in_specs, out_specs=out_specs, check_vma=False)
```

```python
import functools

import jax
import jax.numpy as jnp
import numpy as np
from jax import lax
from jax.experimental import pallas as pl
from jax.experimental.pallas import tpu as pltpu
from jax.sharding import PartitionSpec as P

MODES = 9
CBANDS = 6
VBANDS = 4
BANDS = CBANDS * VBANDS
ROWS = MODES * 2 * BANDS

broadening = 0.1
MESH = pl.DeviceIdType.MESH


LANES = 128
ENTRIES = 16
CHUNKS = 4


def compact_index():
    index = np.full((CBANDS + VBANDS, LANES), -1, np.int32)
    lane = np.arange(2 * MODES * CBANDS)
    for d in range(CBANDS):
        index[d, : lane.size] = lane * CBANDS + d
    lane = np.arange(2 * MODES * VBANDS)
    for w in range(VBANDS):
        index[CBANDS + w, : lane.size] = 2 * MODES * CBANDS * CBANDS + lane * VBANDS + w
    return index


def compact_tables(table):
    index = compact_index()
    count, kpoints, size = table.shape
    select = (jnp.arange(size, dtype=jnp.int32)[:, None] == jnp.asarray(index).reshape(1, -1)).astype(table.dtype)
    rows = jnp.dot(table.reshape(count * kpoints, size), select).reshape(count, kpoints, index.shape[0], LANES)
    return rows.reshape(count, kpoints * index.shape[0], LANES)


def pad_table():
    row = np.arange(ENTRIES * ENTRIES)
    kept = row % ENTRIES < CBANDS + VBANDS
    pad = np.zeros((row.size, ENTRIES * (CBANDS + VBANDS)), np.float32)
    pad[row[kept], (row // ENTRIES * (CBANDS + VBANDS) + row % ENTRIES)[kept]] = 1
    return pad


def lane_tables():
    u, pout, c, v = np.unravel_index(np.arange(ROWS), (MODES, 2, CBANDS, VBANDS))
    padded_rows = -(-ROWS // LANES) * LANES
    electron = np.zeros((LANES, 2, padded_rows), np.float32)
    hole = np.zeros((LANES, 2, padded_rows), np.float32)
    for pin in range(2):
        part = pout ^ pin
        electron[(part * MODES + u) * CBANDS + c, pin, np.arange(ROWS)] = 1
        hole[(part * MODES + u) * VBANDS + v, pin, np.arange(ROWS)] = 1
    return electron.reshape(LANES, -1), hole.reshape(LANES, -1)


def spread_tables():
    u, pout, c, v = np.unravel_index(np.arange(ROWS), (MODES, 2, CBANDS, VBANDS))
    spread = np.zeros((4 * BANDS, 2 * ENTRIES), np.float32)
    mask = np.zeros((4 * BANDS, -(-ROWS // LANES) * LANES), np.float32)
    row = 0
    for hole in range(2):
        for pin in range(2):
            sign = np.where((pout == 0) & (pin == 1), -1.0, 1.0)
            for band in range(CBANDS):
                for other in range(VBANDS):
                    spread[row, pin * ENTRIES + (CBANDS + other if hole else band)] = 1
                    mask[row, :ROWS] = -sign * (c == band) if hole else sign * (v == other)
                    row += 1
    return spread, mask


def greet(workers, parts):
    worker, part = lax.axis_index("wide"), lax.axis_index("narrow")
    barrier = pltpu.get_barrier_semaphore()
    me = worker * parts + part
    total = workers * parts

    def hello(step, carry):
        other = lax.rem(me + step, total)
        pl.semaphore_signal(
            barrier, inc=1, device_id={"wide": other // parts, "narrow": lax.rem(other, parts)}, device_id_type=MESH
        )
        return carry

    lax.fori_loop(1, total, hello, 0)
    pl.semaphore_wait(barrier, total - 1)


def to_all(workers, parts, source, landing, send_sem, recv_sem, wait):
    worker, part = lax.axis_index("wide"), lax.axis_index("narrow")
    me = worker * parts + part
    total = workers * parts

    def one(step, carry):
        other = lax.rem(me + step, total)
        copy = pltpu.make_async_remote_copy(
            src_ref=source,
            dst_ref=landing.at[me],
            send_sem=send_sem.at[step],
            recv_sem=recv_sem.at[step],
            device_id={"wide": other // parts, "narrow": lax.rem(other, parts)},
            device_id_type=MESH,
        )
        if wait:
            copy.wait()
        else:
            copy.start()
        return carry

    lax.fori_loop(1, total, one, 0)


def exchange_kernel(workers, parts, energy_ref, pair_ref, small_out, mine, smalls, s_send, s_recv):
    worker, part = lax.axis_index("wide"), lax.axis_index("narrow")
    owned, slots = energy_ref.shape[0], pair_ref.shape[0]
    mine[...] = jnp.zeros(mine.shape, mine.dtype)
    mine[:owned] = energy_ref[...].astype(jnp.float32)
    mine[owned : owned + slots, :2] = pair_ref[...].astype(jnp.float32)
    greet(workers, parts)
    to_all(workers, parts, mine, smalls, s_send, s_recv, False)
    smalls[worker * parts + part] = mine[...]
    to_all(workers, parts, mine, smalls, s_send, s_recv, True)
    small_out[...] = smalls[...]


def exchange(workers, parts, energies, pairs):
    total = workers * parts
    shape = (energies.shape[0] + pairs.shape[0], energies.shape[1])
    return pl.pallas_call(
        functools.partial(exchange_kernel, workers, parts),
        in_specs=[pl.BlockSpec(memory_space=pltpu.VMEM)] * 2,
        out_specs=pl.BlockSpec(memory_space=pltpu.VMEM),
        out_shape=jax.ShapeDtypeStruct((total,) + shape, jnp.float32),
        scratch_shapes=[
            pltpu.VMEM(shape, jnp.float32),
            pltpu.VMEM((total,) + shape, jnp.float32),
            pltpu.SemaphoreType.DMA((total,)),
            pltpu.SemaphoreType.DMA((total,)),
        ],
        compiler_params=pltpu.CompilerParams(collective_id=0, has_side_effects=True),
    )(energies, pairs)


def rate_kernel(
    workers, parts, index_ref, omega_ref, table_ref, coeffs_ref, pad_ref, electron_ref, hole_ref, spread_ref,
    mask_ref, small_ref, out_ref, *scratch,
):
    wholes, scratch = scratch[:CHUNKS], scratch[CHUNKS:]
    (
        tables, picked, near, staged, distant, mixed, partial, rates, gathered, w_send, w_recv, f_send, f_recv,
        t_send, t_recv, tf_send, tf_recv, n_send, n_recv, m_send, m_recv, r_send, r_recv,
    ) = scratch
    worker, part = lax.axis_index("wide"), lax.axis_index("narrow")
    me = worker * parts + part
    half, chips = parts // 2, workers // 2
    chip, core = worker // 2, lax.rem(worker, 2)
    partner = chip * 2 + 1 - core
    side, place = part // half, lax.rem(part, half)
    share = index_ref.shape[0]
    owned, _, columns, trans = coeffs_ref.shape
    chunk = trans // CHUNKS
    width = half * columns
    count = table_ref.shape[0]
    table_half = table_ref.shape[1] // 2
    steps = chunk // (2 * BANDS)

    def remote(src, dst, send, recv, device):
        return pltpu.make_async_remote_copy(
            src_ref=src, dst_ref=dst, send_sem=send, recv_sem=recv, device_id=device, device_id_type=MESH
        )

    def block(c, owner):
        return wholes[c].at[pl.ds(owner * owned, owned)]

    def wide_copy(c, hop):
        source = coeffs_ref.at[:, :, :, pl.ds(c * chunk, chunk)]
        target = partner if hop == 0 else lax.rem(chip + hop, chips) * 2 + core
        return remote(source, block(c, worker), w_send.at[c, hop], w_recv.at[c, hop], {"wide": target})

    def arrived(hop):
        return partner if hop == 0 else lax.rem(chip - hop + chips, chips) * 2 + core

    def wide_wait(c, hop):
        landing = block(c, arrived(hop))
        return remote(landing, landing, w_send.at[c, hop], w_recv.at[c, hop], {"wide": partner})

    def forward(c, hop):
        landing = block(c, arrived(hop))
        return remote(landing, landing, f_send.at[c, hop], f_recv.at[c, hop], {"wide": partner})

    def forward_wait(c, hop):
        landing = block(c, lax.rem(chip - hop + chips, chips) * 2 + 1 - core)
        return remote(landing, landing, f_send.at[c, hop], f_recv.at[c, hop], {"wide": partner})

    def table_rows(owner, which):
        start = pl.multiple_of(which * table_half, table_half)
        return tables.at[pl.ds(owner * count, count), pl.ds(start, table_half)]

    def table_copy(step):
        start = pl.multiple_of(core * table_half, table_half)
        return remote(
            table_ref.at[:, pl.ds(start, table_half)], table_rows(part, core), t_send.at[step], t_recv.at[step],
            {"narrow": lax.rem(part + step, parts)},
        )

    def table_arrival(step, which, send, recv):
        landing = table_rows(lax.rem(part - step + parts, parts), which)
        return remote(landing, landing, send.at[step], recv.at[step], {"wide": partner})

    def rows_of(c):
        return pl.ds(c * chunk, chunk)

    def near_copy(pair, c, i):
        ref = near.at[pair, place, :, rows_of(c)]
        return remote(ref, ref, n_send.at[pair, c, i], n_recv.at[pair, c, place], {"narrow": side * half + i})

    def near_wait(pair, c, i):
        ref = near.at[pair, i, :, rows_of(c)]
        return remote(ref, ref, n_send.at[pair, c, i], n_recv.at[pair, c, i], {"narrow": side * half + i})

    def far_copy(pair, c, t):
        slot = lax.rem(part, 2)
        return remote(
            staged.at[pair, :, :, rows_of(c)], distant.at[pair, slot, :, :, rows_of(c)],
            m_send.at[pair, c, t], m_recv.at[pair, c, slot], {"narrow": t * half + part // 2},
        )

    def far_wait(pair, c, s):
        ref = distant.at[pair, s, :, :, rows_of(c)]
        return remote(ref, ref, m_send.at[pair, c, s], m_recv.at[pair, c, s], {"narrow": place * 2 + s})

    def stage_near(pair, c):
        rows = wholes[c][index_ref[pair, 0]]
        for p in range(2):
            near[pair, place, p, rows_of(c)] = rows[p].T
        for i in range(half):
            pl.when(side * half + i != part)(near_copy(pair, c, i).start)

    def stage_far(pair, c):
        rows = wholes[c][index_ref[pair, 1]]
        staged[pair, :, :, rows_of(c)] = rows
        for t in range(2):
            target = t * half + part // 2
            pl.when(target != part)(far_copy(pair, c, t).start)

            @pl.when(target == part)
            def _():
                distant[pair, lax.rem(part, 2), :, :, rows_of(c)] = rows

    def pick(pair):
        size, kept = pad_ref.shape
        lanes = 2 * mask_ref.shape[1]

        def some(step, carry):
            rows = pl.ds(pl.multiple_of(step * size, size), size)
            packed = tables[index_ref[pair, 2], pl.ds(pl.multiple_of(step * kept, kept), kept)]
            entries = jnp.dot(pad_ref[...], packed, preferred_element_type=jnp.float32).astype(jnp.bfloat16)
            electron = jnp.dot(entries, electron_ref[...], preferred_element_type=jnp.float32)
            hole = jnp.dot(entries, hole_ref[...], preferred_element_type=jnp.float32)
            entry = lax.rem(lax.broadcasted_iota(jnp.int32, (size, lanes), 0), ENTRIES)
            picked[pair, rows] = jnp.where(entry < CBANDS, electron, hole).astype(jnp.bfloat16)
            return carry

        lax.fori_loop(0, table_ref.shape[1] // kept, some, 0)

    def mix(pair, c):
        for i in range(half):
            pl.when(side * half + i != part)(near_wait(pair, c, i).wait_recv)
        lanes = mask_ref.shape[1]

        def some(step, carry):
            start = pl.multiple_of(step * 2 * BANDS, 2 * BANDS)
            whole_rows = [
                jnp.concatenate([near[pair, i, p, pl.ds(start, 2 * BANDS)] for i in range(half)], axis=1).astype(
                    jnp.float32
                )
                for p in range(2)
            ]
            blocks = []
            for offset in range(2):
                first = pl.multiple_of((step * 2 + offset) * ENTRIES, ENTRIES)
                entries = picked[pair, pl.ds(first, ENTRIES)]
                entries = jnp.concatenate([entries[:, :lanes], entries[:, lanes:]], axis=0)
                spread = jnp.dot(spread_ref[...], entries, preferred_element_type=jnp.float32)
                gain = (spread.astype(jnp.bfloat16) * mask_ref[...])[:, :ROWS]
                rows = jnp.concatenate([part_rows[offset * BANDS : (offset + 1) * BANDS] for part_rows in whole_rows], axis=0)
                rows = rows.astype(jnp.bfloat16)
                rows = jnp.concatenate([rows, rows], axis=0)
                blocks.append(
                    lax.dot_general(gain, rows, (((0,), (0,)), ((), ())), preferred_element_type=jnp.float32)
                )
            for u in range(MODES):
                for p in range(2):
                    low = (u * 2 + p) * BANDS
                    both = jnp.concatenate([one[low : low + BANDS] for one in blocks], axis=0)
                    mixed[u, pl.ds(start, 2 * BANDS), p * width : (p + 1) * width] = both.astype(jnp.bfloat16)
            return carry

        lax.fori_loop(c * steps, (c + 1) * steps, some, 0)

    def gap_of(pair):
        own = [small_ref[index_ref[pair, 3] + side * half + i, pl.ds(index_ref[pair, 4], 1)] for i in range(half)]
        own = jnp.concatenate(own, axis=1)
        far = []
        for s in range(2):
            row = small_ref[index_ref[pair, 5] + place * 2 + s, pl.ds(index_ref[pair, 6], 1)]
            column = jnp.broadcast_to(row, (columns, columns)).T
            far.append(jnp.concatenate([column] * half, axis=1))
        return jnp.concatenate(far, axis=0) - own

    def far_arrival(pair, first, last):
        for c in range(first, last):
            for s in range(2):
                pl.when(place * 2 + s != part)(far_wait(pair, c, s).wait_recv)

    def weigh(pair, u, coupled, gap):
        coupled = coupled.reshape(2, 2, columns, 2 * width)
        real = coupled[:, 0, :, :width] + coupled[:, 1, :, width:]
        imag = coupled[:, 0, :, width:] - coupled[:, 1, :, :width]
        scaled = (gap - omega_ref[index_ref[pair, 2], u]) / broadening
        power = (real * real + imag * imag).reshape(2 * columns, width) / (1.0 + scaled * scaled)
        return jnp.sum(power, axis=0, keepdims=True)

    def couple(pair):
        cut = trans // 2
        gap = gap_of(pair)
        far_arrival(pair, 0, CHUNKS // 2)

        def start(u, carry):
            far_rows = distant[pair, :, :, :, :cut].reshape(4 * columns, cut)
            partial[u] = jnp.dot(far_rows, mixed[u, :cut], preferred_element_type=jnp.float32)
            return carry

        lax.fori_loop(0, MODES, start, 0)
        far_arrival(pair, CHUNKS // 2, CHUNKS)

        def finish(u, total):
            far_rows = distant[pair, :, :, :, cut:].reshape(4 * columns, trans - cut)
            coupled = partial[u] + jnp.dot(far_rows, mixed[u, cut:], preferred_element_type=jnp.float32)
            return total + weigh(pair, u, coupled, gap)

        rates[pair] = lax.fori_loop(0, MODES, finish, jnp.zeros((1, width), jnp.float32))

    greet(workers, parts)
    for c in range(CHUNKS):
        for hop in range(chips):
            wide_copy(c, hop).start()
    for step in range(1, parts):
        table_copy(step).start()
    for c in range(CHUNKS):
        wholes[c][pl.ds(worker * owned, owned)] = coeffs_ref[:, :, :, rows_of(c)]
    tables[pl.ds(part * count, count)] = table_ref[...]

    for c in range(CHUNKS):
        for hop in range(1, chips):
            wide_wait(c, hop).wait_recv()
            forward(c, hop).start()
        wide_wait(c, 0).wait_recv()
        for hop in range(1, chips):
            forward_wait(c, hop).wait_recv()
        stage_near(0, c)
        stage_far(0, c)
        if c == 0:
            for pair in range(1, share):
                stage_far(pair, 0)
            for step in range(1, parts):
                table_arrival(step, core, t_send, t_recv).wait_recv()
                table_arrival(step, core, tf_send, tf_recv).start()
        if c == 1:
            for step in range(1, parts):
                table_arrival(step, 1 - core, tf_send, tf_recv).wait_recv()
            for pair in range(share):
                pick(pair)
        if c == 2:
            mix(0, 0)
    for pair in range(1, share):
        for c in range(CHUNKS):
            stage_near(pair, c)
        for c in range(1, CHUNKS):
            stage_far(pair, c)
    for c in range(1, CHUNKS):
        mix(0, c)
    couple(0)
    for pair in range(1, share):
        for c in range(CHUNKS):
            mix(pair, c)
        couple(pair)

    gathered[me] = rates[...]
    to_all(workers, parts, rates, gathered, r_send, r_recv, False)
    for c in range(CHUNKS):
        for hop in range(chips):
            wide_copy(c, hop).wait_send()
            if hop:
                forward(c, hop).wait_send()
        for pair in range(share):
            for i in range(half):
                pl.when(side * half + i != part)(near_copy(pair, c, i).wait_send)
            for t in range(2):
                pl.when(t * half + part // 2 != part)(far_copy(pair, c, t).wait_send)
    for step in range(1, parts):
        table_copy(step).wait_send()
        table_arrival(step, core, tf_send, tf_recv).wait_send()
    to_all(workers, parts, rates, gathered, r_send, r_recv, True)
    out_ref[...] = gathered[...]


def pair_rates(workers, parts, index, omega, table, coeffs, small):
    share = index.shape[0]
    owned, _, columns, trans = coeffs.shape
    total, half, chips = workers * parts, parts // 2, workers // 2
    width = half * columns
    electron, hole = lane_tables()
    spread, mask = spread_tables()
    constants = [jnp.asarray(one, jnp.bfloat16) for one in (pad_table(), electron, hole, spread, mask)]
    flops = 2 * share * (trans // BANDS * 4 * BANDS * ROWS * width + 8 * columns * trans * MODES * width)
    smem, vmem = pl.BlockSpec(memory_space=pltpu.SMEM), pl.BlockSpec(memory_space=pltpu.VMEM)
    dma, bf16 = pltpu.SemaphoreType.DMA, jnp.bfloat16
    return pl.pallas_call(
        functools.partial(rate_kernel, workers, parts),
        in_specs=[smem, smem] + [vmem] * 8,
        out_specs=vmem,
        out_shape=jax.ShapeDtypeStruct((total, share, 1, width), jnp.float32),
        scratch_shapes=[pltpu.VMEM((owned * workers, 2, columns, trans // CHUNKS), bf16)] * CHUNKS
        + [
            pltpu.VMEM((table.shape[0] * parts,) + table.shape[1:], bf16),
            pltpu.VMEM((share, trans // BANDS * ENTRIES, electron.shape[1]), bf16),
            pltpu.VMEM((share, half, 2, trans, columns), bf16),
            pltpu.VMEM((share, 2, columns, trans), bf16),
            pltpu.VMEM((share, 2, 2, columns, trans), bf16),
            pltpu.VMEM((MODES, trans, 2 * width), bf16),
            pltpu.VMEM((MODES, 4 * columns, 2 * width), jnp.float32),
            pltpu.VMEM((share, 1, width), jnp.float32),
            pltpu.VMEM((total, share, 1, width), jnp.float32),
        ]
        + [dma((CHUNKS, chips))] * 4
        + [dma((parts,))] * 4
        + [dma((share, CHUNKS, half))] * 2
        + [dma((share, CHUNKS, 2))] * 2
        + [dma((total,))] * 2,
        compiler_params=pltpu.CompilerParams(
            collective_id=1, has_side_effects=True, vmem_limit_bytes=60 * 1024 * 1024
        ),
        cost_estimate=pl.CostEstimate(flops=flops, bytes_accessed=4 * coeffs.size, transcendentals=0),
    )(index, omega, table, coeffs, *constants, small)


def shards(coeffs, energies, g_coupling, omega, pairs, counts, blocks):
    worker = lax.axis_index("wide")
    part = lax.axis_index("narrow")
    workers = lax.axis_size("wide")
    owned, _, columns, trans = coeffs.shape
    momenta = owned * workers
    slots = pairs.shape[0]
    excitons = blocks.shape[1]

    parts = lax.axis_size("narrow")
    small = exchange(workers, parts, energies, pairs)
    listed = small.reshape(workers, parts, owned + slots, columns)[:, 0, owned:, :2]

    before = jnp.arange(workers)[:, None] > jnp.arange(workers)[None, :]
    rank = jnp.sum(jnp.where(before, counts[None, :], 0), axis=1)[:, None] + jnp.arange(slots)[None, :]
    rank = jnp.where(jnp.arange(slots)[None, :] < counts[:, None], rank, -1)

    def live_rows(wanted):
        hit = (rank[None, :, :] == wanted[:, None, None])[..., None]
        return jnp.sum(jnp.where(hit, listed[None], 0.0), axis=(1, 2)).astype(jnp.int32)

    mine = live_rows(worker * owned + jnp.arange(owned))
    home, shift = mine[:, 0], mine[:, 1]
    far_index = (home + shift) % momenta
    index = jnp.stack(
        [
            home, far_index, shift,
            home // owned * parts, home % owned, far_index // owned * parts, far_index % owned,
        ],
        axis=1,
    )
    rates = pair_rates(workers, parts, index, omega, compact_tables(g_coupling), coeffs, small)

    live_home = live_rows(jnp.arange(momenta))[:, 0]
    half = parts // 2
    rates = rates.reshape(workers, 2, half, owned, half * columns).sum(axis=2)
    rates = rates.transpose(0, 2, 1, 3).reshape(momenta, excitons)
    local = worker * owned + jnp.arange(owned)
    chosen = (live_home[None, :] == local[:, None]).astype(jnp.float32)
    total = jnp.sum(chosen[:, :, None] * rates[None, :, :], axis=1)
    margin = 3
    widened = jnp.pad(total, ((0, 0), (margin, margin)))
    padded_labels = jnp.pad(blocks, ((0, 0), (margin, margin)), constant_values=-1)
    widened = lax.dynamic_slice_in_dim(widened, part * columns, columns + 2 * margin, 1)
    near_labels = lax.dynamic_slice_in_dim(padded_labels, part * columns, columns + 2 * margin, 1)
    my_labels = near_labels[:, margin : margin + columns]
    upper = jnp.zeros((owned, columns), jnp.float32)
    lower = jnp.zeros((owned, columns), jnp.float32)
    for offset in range(2 * margin + 1):
        same = (near_labels[:, offset : offset + columns] == my_labels).astype(jnp.float32)
        upper += same * widened[:, offset : offset + columns]
        lower += same
    return upper / lower


def solution(mesh):
    in_specs = (
        P(("groups", "wide"), None, "narrow", None),
        P(("groups", "wide"), "narrow"),
        P(("groups", "narrow"), None, None),
        P("groups", None),
        P(("groups", "wide"), None),
        P("groups"),
        P(("groups", "wide"), None),
    )
    out_specs = P(("groups", "wide"), "narrow")
    return jax.shard_map(shards, mesh=mesh, in_specs=in_specs, out_specs=out_specs, check_vma=False)
```
